32 devices in a mesh: seq: 4 (over y, x), dp: 8 (over z, core).
Axes of the slice: x: 2, y: 2, z: 4, core: 2. Of those that a mesh axis runs over, the one named last changes fastest.
Arguments:
- tokens: bfloat16 [8, 768, 1408], P('dp', 'seq')
- qkv_weight: bfloat16 [1408, 2112], replicated
- grad_out: bfloat16 [8, 768, 704], P('dp', 'seq'), may hold values from -6 to 6
- keep: int32 [8, 128], P('dp'), may hold values from 0 to 1023, as said below
Outputs:
- grad_tokens: bfloat16 [8, 768, 1408], P('dp', 'seq')
- grad_weight: float32 [1408, 2112], P(('seq', 'dp'))
The draws below stay inside these ranges and needn't reach their ends.
Inputs may be any that keep to these rules, and one draw needn't show every extreme that they name: `keep`: each row holds 128 different spatial positions below 1024, in increasing order.
All inputs are finite; a program needn't handle non-finite values.
Results may differ from the reference program's by a relative error of at most 0.03.
Values may be sent and summed in bfloat16 or wider, within the bound.
A program may use at most 64 MiB of HBM per device.

```python
import jax
import jax.numpy as jnp
from jax import lax

D = 1408
HEADS = 8
HEAD_DIM = 88
GRID = 1024
VIS = 128
ATT = 704
SEQ = 768
CLIPS = 8


def draw_tokens(key, part):
    key = jax.random.fold_in(key, 11)
    first = jax.random.fold_in(key, 0)
    base = jnp.clip(jax.random.normal(first, (CLIPS, SEQ, D), jnp.float32), -6.0, 6.0)
    return base.astype(jnp.bfloat16)


def draw_qkv_weight(key, part):
    key = jax.random.fold_in(key, 12)
    base = jnp.clip(jax.random.normal(key, (D, 3 * ATT), jnp.float32), -6.0, 6.0) * D ** (-0.5)
    return base.astype(jnp.bfloat16)


def draw_keep(key, part):
    key = jax.random.fold_in(key, 13)
    keys = jax.random.split(key, CLIPS)

    def one_row(row_key):
        order = jax.random.permutation(row_key, GRID)
        picked = jnp.argsort(order)[:VIS]
        return jnp.sort(picked).astype(jnp.int32)
    return jax.vmap(one_row)(keys)


def steps_of(own_key, dims, pieces, low, largest):
    factor_of = 1.0
    for position, parts in pieces:
        heights = jax.random.uniform(jax.random.fold_in(jax.random.fold_in(own_key, 6), position), (parts,), jnp.float32, low / len(pieces), largest / len(pieces))
        factor_of = factor_of * jnp.repeat(jnp.exp(heights), dims[position] // parts).reshape((-1,) + (1,) * (len(dims) - 1 - position))
    return factor_of


def noise(rng, dims, spread, reach, cuts=(), kind=jnp.bfloat16):
    drawn = spread * jax.random.normal(rng, dims, jnp.float32)
    if cuts:
        drawn = drawn * steps_of(rng, dims, cuts, -0.22, 0.18)
    return jnp.clip(drawn, -reach, reach).astype(kind)


def setup_inputs(seed: int = 0) -> dict:
    seeds = jax.random.split(jax.random.key(seed), 5)
    return {
        "tokens": draw_tokens(jax.random.fold_in(seeds[4], 71), 0),
        "qkv_weight": draw_qkv_weight(jax.random.fold_in(seeds[4], 71), 0),
        "grad_out": noise(seeds[2], (CLIPS, SEQ, ATT), 1.0, 6.0, ((0, 8), (1, 4))),
        "keep": draw_keep(jax.random.fold_in(seeds[4], 71), 0),
    }


def position_code(rowid, keep_row, width):
    visible = keep_row.shape[0]
    frame = rowid // visible
    slot = rowid % visible
    onehot = slot[:, None] == jnp.arange(visible, dtype=jnp.int32)[None, :]
    spatial = jnp.sum(jnp.where(onehot, keep_row[None, :], 0), axis=1).astype(jnp.int32)
    index = (frame * GRID + spatial).astype(jnp.float32)
    column = jnp.arange(width, dtype=jnp.int32)
    half = (column // 2).astype(jnp.float32)
    inverse = jnp.exp(-(2.0 * half / width) * jnp.log(10000.0))
    angle = index[:, None] * inverse[None, :]
    return jnp.where((column % 2 == 0)[None, :], jnp.sin(angle), jnp.cos(angle))


def attend(queries, keys, values, grads):
    length = queries.shape[0]
    scale = HEAD_DIM ** -0.5
    block = 512 if length % 512 == 0 else length
    count = length // block

    def step(carry, index):
        key_acc, value_acc = carry
        start = index * block
        q_block = lax.dynamic_slice_in_dim(queries, start, block, 0)
        g_block = lax.dynamic_slice_in_dim(grads, start, block, 0)
        scores = jnp.einsum("qhd,khd->hqk", q_block, keys, preferred_element_type=jnp.float32) * scale
        top = jnp.max(scores, axis=-1, keepdims=True)
        expo = jnp.exp(scores - top)
        probs = expo / jnp.sum(expo, axis=-1, keepdims=True)
        weights = probs.astype(jnp.bfloat16)
        attended = jnp.einsum("hqk,khd->qhd", weights, values, preferred_element_type=jnp.float32)
        delta = jnp.sum(g_block.astype(jnp.float32) * attended, axis=-1)
        dprobs = jnp.einsum("qhd,khd->hqk", g_block, values, preferred_element_type=jnp.float32)
        dscores = (probs * (dprobs - jnp.transpose(delta)[:, :, None])).astype(jnp.bfloat16)
        grad_q = (jnp.einsum("hqk,khd->qhd", dscores, keys, preferred_element_type=jnp.float32) * scale).astype(jnp.bfloat16)
        key_acc = key_acc + jnp.einsum("hqk,qhd->khd", dscores, q_block, preferred_element_type=jnp.float32)
        value_acc = value_acc + jnp.einsum("hqk,qhd->khd", weights, g_block, preferred_element_type=jnp.float32)
        return (key_acc, value_acc), grad_q

    zeros = jnp.zeros(keys.shape, jnp.float32)
    (key_acc, value_acc), grad_blocks = lax.scan(step, (zeros, zeros), jnp.arange(count, dtype=jnp.int32))
    grad_q = grad_blocks.reshape(queries.shape)
    grad_k = (key_acc * scale).astype(jnp.bfloat16)
    grad_v = value_acc.astype(jnp.bfloat16)
    return grad_q, grad_k, grad_v


def reference(tokens, qkv_weight, grad_out, keep):
    width = tokens.shape[2]
    length = tokens.shape[1]
    attw = qkv_weight.shape[1] // 3

    def one_clip(total, item):
        clip_tokens, clip_grads, keep_row = item
        code = position_code(jnp.arange(length, dtype=jnp.int32), keep_row, width)
        inputs = (clip_tokens.astype(jnp.float32) + code).astype(jnp.bfloat16)
        qkv = jnp.dot(inputs, qkv_weight, preferred_element_type=jnp.float32).astype(jnp.bfloat16)
        queries = qkv[:, :attw].reshape(length, HEADS, HEAD_DIM)
        keys = qkv[:, attw:2 * attw].reshape(length, HEADS, HEAD_DIM)
        values = qkv[:, 2 * attw:].reshape(length, HEADS, HEAD_DIM)
        grads = clip_grads.reshape(length, HEADS, HEAD_DIM)
        grad_q, grad_k, grad_v = attend(queries, keys, values, grads)
        grad_qkv = jnp.concatenate([grad_q.reshape(length, attw), grad_k.reshape(length, attw), grad_v.reshape(length, attw)], axis=1)
        grad_tokens = jnp.dot(grad_qkv, jnp.transpose(qkv_weight), preferred_element_type=jnp.float32).astype(jnp.bfloat16)
        term = lax.dot_general(inputs, grad_qkv, (((0,), (0,)), ((), ())), preferred_element_type=jnp.float32)
        return total + term, grad_tokens

    start = jnp.zeros((width, 3 * attw), jnp.float32)
    grad_weight, grad_tokens = lax.scan(one_clip, start, (tokens, grad_out, keep))
    return grad_tokens, grad_weight
```

```python
import functools

import numpy as np
import jax
import jax.numpy as jnp
from jax import lax
from jax.experimental import pallas as pl
from jax.experimental.pallas import tpu as pltpu
from jax.sharding import PartitionSpec as P

HEAD_DIM = 88
GRID = 1024
MESH = pl.DeviceIdType.MESH
LANES = 128
SINE = (
    6.283182793407034,
    -41.34141938561695,
    81.59613875537907,
    -76.57968785099001,
    41.203743633541215,
    -12.268859940824616,
)
NT = (((1,), (1,)), ((), ()))
NN = (((1,), (0,)), ((), ()))


def mm(a, b, dims=NN):
    return lax.dot_general(a, b, dims, preferred_element_type=jnp.float32)


def fused_kernel(
    nz, heads, tokens, weight, grads, keep, freq, phase, gt_out, gw_out,
    x_all, g_send, g_all, w_own, qkv, x_t, dk_acc, dv_acc, d_own, d_back, d_cat,
    dw, part, core_in, pair, z_in, total, last_in,
    x_ss, x_rs, g_ss, g_rs, d_ss, d_rs, c_ss, c_rs, z_ss, z_rs, f_ss, f_rs,
):
    hd = HEAD_DIM
    pairw = 2 * hd
    rows, width = tokens.shape
    attw = weight.shape[1] // 3
    seq = heads // 2
    length = seq * rows
    own_rows = gw_out.shape[0]
    pad_rows = total.shape[1]
    cw = d_own.shape[1]
    visible = keep.shape[1]
    s = lax.axis_index("seq")
    d = lax.axis_index("dp")
    z = d // 2
    c = d % 2
    oc = 1 - c
    sib = z * 2 + oc
    peers = (s + 1 - 2 * (s % 2), (s + 2) % 4, 3 - s)
    zpeers = [(z + k) % nz for k in range(1, nz)]
    zsrcs = [(z + nz - k) % nz for k in range(1, nz)]

    def at_rows(who):
        return pl.ds(pl.multiple_of(who * rows, 64), rows)

    def send(src, dst, ss, rs, dev):
        copy = pltpu.make_async_remote_copy(
            src_ref=src, dst_ref=dst, send_sem=ss, recv_sem=rs,
            device_id=dev, device_id_type=MESH,
        )
        copy.start()
        return copy

    barrier = pltpu.get_barrier_semaphore()
    for p in peers:
        pl.semaphore_signal(barrier, inc=1, device_id=(p, d), device_id_type=MESH)
    pl.semaphore_signal(barrier, inc=1, device_id=(s, sib), device_id_type=MESH)
    for p in zpeers:
        pl.semaphore_signal(barrier, inc=1, device_id=(s, p * 2 + c), device_id_type=MESH)

    row = s * rows + lax.broadcasted_iota(jnp.int32, (rows, visible), 0)
    frame = row // visible
    slot = row - frame * visible
    lane = lax.broadcasted_iota(jnp.int32, (rows, visible), 1)
    spot = jnp.where(slot == lane, (frame * GRID + keep[...]).astype(jnp.float32), 0.0)
    index = jnp.sum(spot, axis=1, keepdims=True)
    mine = at_rows(s)
    half = rows // 2
    x_copies = []
    for part_i in range(2):
        lo = part_i * half
        turns = index[lo : lo + half] * freq[...] + phase[...]
        r = turns - jnp.floor(turns + 0.5)
        r2 = r * r
        poly = jnp.full_like(r2, SINE[-1])
        for coef in SINE[-2::-1]:
            poly = poly * r2 + coef
        x = (tokens[lo : lo + half, :].astype(jnp.float32) + poly * r).astype(jnp.bfloat16)
        where = pl.ds(pl.multiple_of(s * rows + lo, 32), half)
        x_all[where, :] = x
        if part_i == 0:
            pl.semaphore_wait(barrier, 4 + nz - 1)
        for k, p in enumerate(peers):
            x_copies.append(
                send(x_all.at[where], x_all.at[where], x_ss.at[part_i, k], x_rs.at[part_i, k], (p, d))
            )

    g_send[...] = jnp.zeros_like(g_send)
    for p in range(seq):
        for h in range(2):
            g_send[p, :, h * LANES : h * LANES + hd] = grads[:, p * pairw + h * hd : p * pairw + (h + 1) * hd]
    g_copies = [
        send(g_send.at[p], g_all.at[mine], g_ss.at[k], g_rs.at[k], (p, d)) for k, p in enumerate(peers)
    ]
    g_all[mine, :] = g_send[s]

    w_own[...] = jnp.zeros_like(w_own)
    for j in range(seq):

        @pl.when(s == j)
        def _():
            for i in range(3):
                for h in range(2):
                    at = i * attw + j * pairw + h * hd
                    to = (2 * i + h) * LANES
                    w_own[:, to : to + hd] = weight[:, at : at + hd]

    def project(who):
        x = x_all[at_rows(who), :]
        qkv[at_rows(who), :] = mm(x, w_own[...]).astype(jnp.bfloat16)
        x_t[who] = x.T

    project(s)
    for k, p in enumerate(peers):
        for part_i in range(2):
            x_copies[part_i * 3 + k].wait_recv()
        project(p)
    for copy in g_copies:
        copy.wait_recv()

    block = 256 if length % 256 == 0 else rows
    scale = hd ** (-0.5)
    dk_acc[...] = jnp.zeros_like(dk_acc)
    dv_acc[...] = jnp.zeros_like(dv_acc)
    d_own[:, 512:] = jnp.zeros((length, cw - 512), jnp.bfloat16)

    def attention(b, carry):
        at = pl.ds(pl.multiple_of(b * block, block), block)
        for h in range(2):
            q = qkv[at, h * LANES : (h + 1) * LANES]
            g = g_all[at, h * LANES : (h + 1) * LANES]
            keys = qkv[:, (2 + h) * LANES : (3 + h) * LANES]
            values = qkv[:, (4 + h) * LANES : (5 + h) * LANES]
            st = mm(keys, q, NT) * scale
            e = jnp.exp(st - jnp.max(st, axis=0, keepdims=True))
            p = e * (1.0 / jnp.sum(e, axis=0, keepdims=True))
            w = p.astype(jnp.bfloat16)
            dp = mm(values, g, NT)
            delta = jnp.sum(w.astype(jnp.float32) * dp, axis=0, keepdims=True)
            ds = (p * (dp - delta)).astype(jnp.bfloat16)
            dv_acc[h] += mm(w, g)
            dk_acc[h] += mm(ds, q)
            dq = mm(keys.T, ds).T * scale
            d_own[at, h * hd : (h + 1) * hd] = dq[:, :hd].astype(jnp.bfloat16)
        return carry

    lax.fori_loop(0, length // block, attention, 0)
    for h in range(2):
        at = pairw + h * hd
        d_own[:, at : at + hd] = (dk_acc[h, :, :hd] * scale).astype(jnp.bfloat16)
        at = 2 * pairw + h * hd
        d_own[:, at : at + hd] = dv_acc[h, :, :hd].astype(jnp.bfloat16)

    d_copies = [
        send(d_own.at[at_rows(p)], d_back.at[s], d_ss.at[k], d_rs.at[k], (p, d)) for k, p in enumerate(peers)
    ]
    d_back[s] = d_own[mine, :]

    dw[width:, :] = jnp.zeros((dw.shape[0] - width, cw), jnp.float32)
    group = width // seq
    for t in range(seq):
        lo = t * group
        acc = mm(x_t[0, lo : lo + group, :], d_own[0:rows, :])
        for q in range(1, seq):
            acc = acc + mm(x_t[q, lo : lo + group, :], d_own[q * rows : (q + 1) * rows, :])
        dw[lo : lo + group, :] = acc
    for t in range(seq):
        for zz in range(nz):
            for cc in range(2):
                at = ((t * nz + zz) * 2 + cc) * own_rows
                part[cc, zz, t * pad_rows : (t + 1) * pad_rows, :] = dw[at : at + pad_rows, :].astype(jnp.bfloat16)
    core_copy = send(part.at[oc], core_in, c_ss, c_rs, (s, sib))
    core_copy.wait_recv()
    z_copies = []
    for k, p in enumerate(zpeers):
        pair[k] = (part[c, p].astype(jnp.float32) + core_in[p].astype(jnp.float32)).astype(jnp.bfloat16)
        z_copies.append(send(pair.at[k], z_in.at[k], z_ss.at[k], z_rs.at[k], (s, p * 2 + c)))

    for copy in d_copies:
        copy.wait_recv()
    for p in range(seq):
        for i in range(3):
            at = i * attw + p * pairw
            d_cat[:, at : at + pairw] = d_back[p, :, i * pairw : (i + 1) * pairw]
    gt_out[...] = mm(d_cat[...], weight[...], NT).astype(jnp.bfloat16)

    acc = part[c, z].astype(jnp.float32) + core_in[z].astype(jnp.float32)
    for k in range(nz - 1):
        z_copies[k].wait_recv()
        acc = acc + z_in[k].astype(jnp.float32)
    acc = acc.astype(jnp.bfloat16)
    for t in range(seq):
        total[t] = acc[t * pad_rows : (t + 1) * pad_rows, :]
    f_copies = [send(total.at[p], last_in.at[s], f_ss.at[k], f_rs.at[k], (p, d)) for k, p in enumerate(peers)]
    last_in[s] = total[s]
    for copy in f_copies:
        copy.wait_recv()
    for p in range(seq):
        for i in range(3):
            at = i * attw + p * pairw
            gw_out[:, at : at + pairw] = last_in[p, :own_rows, i * pairw : (i + 1) * pairw].astype(jnp.float32)
    for copy in x_copies + g_copies + d_copies + [core_copy] + z_copies + f_copies:
        copy.wait_send()


def fused(nz, tokens, qkv_weight, grad_out, keep):
    tokens, grad_out = tokens[0], grad_out[0]
    rows, width = tokens.shape
    cols = qkv_weight.shape[1]
    attw = cols // 3
    heads = attw // HEAD_DIM
    seq = heads // 2
    length = seq * rows
    own_rows = width // (seq * nz * 2)
    pad_rows = -(-own_rows // 16) * 16
    cw = -(-6 * HEAD_DIM // LANES) * LANES
    column = np.arange(width)
    freq = 10000.0 ** (-(2.0 * (column // 2)) / width) / (2.0 * np.pi)
    freq = jnp.asarray(freq[None, :].astype(np.float32))
    phase = jnp.asarray((0.25 * (column % 2))[None, :].astype(np.float32))
    bf16, f32 = jnp.bfloat16, jnp.float32
    vmem = pltpu.VMEM
    dma = pltpu.SemaphoreType.DMA
    scratch = [
        vmem((length, width), bf16),
        vmem((seq, rows, 2 * LANES), bf16),
        vmem((length, 2 * LANES), bf16),
        vmem((width, 6 * LANES), bf16),
        vmem((length, 6 * LANES), bf16),
        vmem((seq, width, rows), bf16),
        vmem((2, length, LANES), f32),
        vmem((2, length, LANES), f32),
        vmem((length, cw), bf16),
        vmem((seq, rows, cw), bf16),
        vmem((rows, cols), bf16),
        vmem((width + 8, cw), f32),
        vmem((2, nz, seq * pad_rows, cw), bf16),
        vmem((nz, seq * pad_rows, cw), bf16),
        vmem((nz - 1, seq * pad_rows, cw), bf16),
        vmem((nz - 1, seq * pad_rows, cw), bf16),
        vmem((seq, pad_rows, cw), bf16),
        vmem((seq, pad_rows, cw), bf16),
        dma((2, 3)), dma((2, 3)), dma((3,)), dma((3,)), dma((3,)), dma((3,)),
        dma, dma, dma((nz - 1,)), dma((nz - 1,)), dma((3,)), dma((3,)),
    ]
    whole = pl.BlockSpec(memory_space=pltpu.VMEM)
    gt, gw = pl.pallas_call(
        functools.partial(fused_kernel, nz, heads),
        out_shape=[
            jax.ShapeDtypeStruct((rows, width), bf16),
            jax.ShapeDtypeStruct((own_rows, cols), f32),
        ],
        in_specs=[whole] * 6,
        out_specs=[whole] * 2,
        scratch_shapes=scratch,
        compiler_params=pltpu.CompilerParams(
            collective_id=0, has_side_effects=True, vmem_limit_bytes=58 * 2**20
        ),
    )(tokens, qkv_weight, grad_out, keep, freq, phase)
    return gt[None], gw


def position_code(rowid, keep_row, width):
    visible = keep_row.shape[0]
    frame = rowid // visible
    slot = rowid % visible
    onehot = slot[:, None] == jnp.arange(visible, dtype=jnp.int32)[None, :]
    spatial = jnp.sum(jnp.where(onehot, keep_row[None, :], 0), axis=1)
    index = (frame * GRID + spatial).astype(jnp.float32)
    column = jnp.arange(width, dtype=jnp.int32)
    half = (column // 2).astype(jnp.float32)
    inverse = jnp.exp(-(2.0 * half / width) * jnp.log(10000.0))
    angle = index[:, None] * inverse[None, :]
    return jnp.where((column % 2 == 0)[None, :], jnp.sin(angle), jnp.cos(angle))


def attend(queries, keys, values, grads):
    length = queries.shape[0]
    scale = HEAD_DIM ** (-0.5)
    block = 512 if length % 512 == 0 else length
    count = length // block

    def step(carry, index):
        key_acc, value_acc = carry
        start = index * block
        q_block = lax.dynamic_slice_in_dim(queries, start, block, 0)
        g_block = lax.dynamic_slice_in_dim(grads, start, block, 0)
        scores = (
            jnp.einsum("qhd,khd->hqk", q_block, keys, preferred_element_type=jnp.float32) * scale
        )
        top = jnp.max(scores, axis=-1, keepdims=True)
        expo = jnp.exp(scores - top)
        probs = expo / jnp.sum(expo, axis=-1, keepdims=True)
        weights = probs.astype(jnp.bfloat16)
        attended = jnp.einsum("hqk,khd->qhd", weights, values, preferred_element_type=jnp.float32)
        delta = jnp.sum(g_block.astype(jnp.float32) * attended, axis=-1)
        dprobs = jnp.einsum("qhd,khd->hqk", g_block, values, preferred_element_type=jnp.float32)
        dscores = (probs * (dprobs - jnp.transpose(delta)[:, :, None])).astype(jnp.bfloat16)
        grad_q = (
            jnp.einsum("hqk,khd->qhd", dscores, keys, preferred_element_type=jnp.float32) * scale
        ).astype(jnp.bfloat16)
        key_acc = key_acc + jnp.einsum(
            "hqk,qhd->khd", dscores, q_block, preferred_element_type=jnp.float32
        )
        value_acc = value_acc + jnp.einsum(
            "hqk,qhd->khd", weights, g_block, preferred_element_type=jnp.float32
        )
        return ((key_acc, value_acc), grad_q)

    zeros = jnp.zeros(keys.shape, jnp.float32)
    (key_acc, value_acc), grad_blocks = lax.scan(
        step, (zeros, zeros), jnp.arange(count, dtype=jnp.int32)
    )
    grad_q = grad_blocks.reshape(queries.shape)
    grad_k = (key_acc * scale).astype(jnp.bfloat16)
    grad_v = value_acc.astype(jnp.bfloat16)
    return (grad_q, grad_k, grad_v)


def weight_term(inputs, grad_qkv):
    return lax.dot_general(
        inputs, grad_qkv, (((0,), (0,)), ((), ())), preferred_element_type=jnp.float32
    )


def local(tokens, qkv_weight, grad_out, keep):
    local_tokens = tokens[0]
    local_grads = grad_out[0]
    rows = local_tokens.shape[0]
    width = local_tokens.shape[1]
    attw = qkv_weight.shape[1] // 3
    rowid = lax.axis_index("seq") * rows + jnp.arange(rows, dtype=jnp.int32)
    code = position_code(rowid, keep[0], width)
    inputs = (local_tokens.astype(jnp.float32) + code).astype(jnp.bfloat16)
    qkv = jnp.dot(inputs, qkv_weight, preferred_element_type=jnp.float32).astype(jnp.bfloat16)
    head_q, head_k, head_v, head_g = (
        lax.all_to_all(qkv[:, :attw], "seq", split_axis=1, concat_axis=0, tiled=True),
        lax.all_to_all(qkv[:, attw : 2 * attw], "seq", split_axis=1, concat_axis=0, tiled=True),
        lax.all_to_all(qkv[:, 2 * attw :], "seq", split_axis=1, concat_axis=0, tiled=True),
        lax.all_to_all(local_grads, "seq", split_axis=1, concat_axis=0, tiled=True),
    )
    length = head_q.shape[0]
    narrow = head_q.shape[1]
    shape = (length, narrow // HEAD_DIM, HEAD_DIM)
    grad_q, grad_k, grad_v = attend(
        head_q.reshape(shape), head_k.reshape(shape), head_v.reshape(shape), head_g.reshape(shape)
    )
    flat_q = grad_q.reshape(length, narrow)
    flat_k = grad_k.reshape(length, narrow)
    flat_v = grad_v.reshape(length, narrow)
    back_q, back_k, back_v = (
        lax.all_to_all(flat_q, "seq", split_axis=0, concat_axis=1, tiled=True),
        lax.all_to_all(flat_k, "seq", split_axis=0, concat_axis=1, tiled=True),
        lax.all_to_all(flat_v, "seq", split_axis=0, concat_axis=1, tiled=True),
    )
    grad_qkv = jnp.concatenate([back_q, back_k, back_v], axis=1)
    grad_tokens = jnp.dot(
        grad_qkv, jnp.transpose(qkv_weight), preferred_element_type=jnp.float32
    ).astype(jnp.bfloat16)
    partial_rows = lax.psum_scatter(
        weight_term(inputs, grad_qkv).astype(jnp.bfloat16), "seq", scatter_dimension=0, tiled=True
    )
    grad_weight = lax.psum_scatter(partial_rows, "dp", scatter_dimension=0, tiled=True).astype(
        jnp.float32
    )
    return (grad_tokens[None], grad_weight)


def solution(mesh):
    in_specs = (P("dp", "seq", None), P(), P("dp", "seq", None), P("dp", None))
    out_specs = (P("dp", "seq", None), P(("seq", "dp"), None))
    seq, dp = mesh.shape["seq"], mesh.shape["dp"]

    def device(tokens, qkv_weight, grad_out, keep):
        heads = qkv_weight.shape[1] // 3 // HEAD_DIM
        rows = tokens.shape[1]
        if seq == 4 and heads == 2 * seq and dp % 2 == 0 and rows % 64 == 0:
            return fused(dp // 2, tokens, qkv_weight, grad_out, keep)
        return local(tokens, qkv_weight, grad_out, keep)

    return jax.shard_map(device, mesh=mesh, in_specs=in_specs, out_specs=out_specs, check_vma=False)
```

```python
import functools

import numpy as np
import jax
import jax.numpy as jnp
from jax import lax
from jax.experimental import pallas as pl
from jax.experimental.pallas import tpu as pltpu
from jax.sharding import PartitionSpec as P

HEAD_DIM = 88
GRID = 1024
MESH = pl.DeviceIdType.MESH
LANES = 128
SINE = (
    6.283182793407034,
    -41.34141938561695,
    81.59613875537907,
    -76.57968785099001,
    41.203743633541215,
    -12.268859940824616,
)
NT = (((1,), (1,)), ((), ()))
NN = (((1,), (0,)), ((), ()))


def mm(a, b, dims=NN):
    return lax.dot_general(a, b, dims, preferred_element_type=jnp.float32)


def fused_kernel(
    nz, heads, tokens, weight, grads, keep, freq, phase, gt_out, gw_out,
    x_all, g_send, g_all, w_own, w_all, qkv, x_t, dk_acc, dv_acc, d_own, d_back, d_cat,
    part, core_in, pair, z_in, total, last_in,
    w_sem, x_ss, x_rs, r_ss, r_rs, g_ss, g_rs, d_ss, d_rs, c_ss, c_rs, z_ss, z_rs, f_ss, f_rs,
):
    hd = HEAD_DIM
    pairw = 2 * hd
    rows, width = tokens.shape
    attw = weight.shape[0] // 3
    seq = heads // 2
    length = seq * rows
    own_rows = gw_out.shape[0]
    pad_rows = total.shape[1]
    cw = d_own.shape[1]
    visible = keep.shape[1]
    s = lax.axis_index("seq")
    d = lax.axis_index("dp")
    z = d // 2
    c = d % 2
    oc = 1 - c
    sib = z * 2 + oc
    peers = (s + 1 - 2 * (s % 2), (s + 2) % 4, 3 - s)
    zpeers = [(z + k) % nz for k in range(1, nz)]
    zsrcs = [(z + nz - k) % nz for k in range(1, nz)]

    def at_rows(who):
        return pl.ds(pl.multiple_of(who * rows, 64), rows)

    def send(src, dst, ss, rs, dev):
        copy = pltpu.make_async_remote_copy(
            src_ref=src, dst_ref=dst, send_sem=ss, recv_sem=rs,
            device_id=dev, device_id_type=MESH,
        )
        copy.start()
        return copy

    w_copies = [
        pltpu.make_async_copy(
            weight.at[pl.ds(pl.multiple_of(i * attw + s * pairw, 16), pairw)], w_own.at[i], w_sem.at[i]
        )
        for i in range(3)
    ]
    w_copies.append(pltpu.make_async_copy(weight, w_all, w_sem.at[3]))
    for copy in w_copies:
        copy.start()

    barrier = pltpu.get_barrier_semaphore()
    for p in peers:
        pl.semaphore_signal(barrier, inc=1, device_id=(p, d), device_id_type=MESH)
    pl.semaphore_signal(barrier, inc=1, device_id=(s, sib), device_id_type=MESH)
    for p in zpeers:
        pl.semaphore_signal(barrier, inc=1, device_id=(s, p * 2 + c), device_id_type=MESH)

    row = s * rows + lax.broadcasted_iota(jnp.int32, (rows, visible), 0)
    frame = row // visible
    slot = row - frame * visible
    lane = lax.broadcasted_iota(jnp.int32, (rows, visible), 1)
    spot = jnp.where(slot == lane, (frame * GRID + keep[...]).astype(jnp.float32), 0.0)
    index = jnp.sum(spot, axis=1, keepdims=True)
    mine = at_rows(s)
    half = rows // 2

    def half_of(who, i):
        return pl.ds(pl.multiple_of(who * rows + i * half, 32), half)

    for i in range(2):
        lo = i * half
        turns = index[lo : lo + half] * freq[...] + phase[...]
        r = turns - jnp.floor(turns + 0.5)
        r2 = r * r
        poly = jnp.full_like(r2, SINE[-1])
        for coef in SINE[-2::-1]:
            poly = poly * r2 + coef
        x = (tokens[lo : lo + half, :].astype(jnp.float32) + poly * r).astype(jnp.bfloat16)
        x_all[half_of(s, i), :] = x
    pl.semaphore_wait(barrier, 4 + nz - 1)
    x_copies = {}
    for k, i in ((0, 0), (1, 1), (0, 1), (1, 0)):
        where = x_all.at[half_of(s, i)]
        x_copies[k, i] = send(where, where, x_ss.at[k, i], x_rs.at[k, i], (peers[k], d))

    g_send[...] = jnp.zeros_like(g_send)
    for p in range(seq):
        for h in range(2):
            g_send[p, :, h * LANES : h * LANES + hd] = grads[:, p * pairw + h * hd : p * pairw + (h + 1) * hd]
    g_copies = [
        send(g_send.at[p], g_all.at[mine], g_ss.at[k], g_rs.at[k], (p, d)) for k, p in enumerate(peers)
    ]
    g_all[mine, :] = g_send[s]

    qkv[...] = jnp.zeros_like(qkv)
    for copy in w_copies[:3]:
        copy.wait()

    def project(who):
        x = x_all[at_rows(who), :]
        for i in range(3):
            out = mm(x, w_own[i], NT).astype(jnp.bfloat16)
            for h in range(2):
                to = (2 * i + h) * LANES
                qkv[at_rows(who), to : to + hd] = out[:, h * hd : (h + 1) * hd]

    def transpose(who):
        xt = x_all[at_rows(who), :].astype(jnp.float32).T
        for r in range(width // own_rows):
            t, zc = r // (2 * nz), r % (2 * nz)
            piece = xt[r * own_rows : (r + 1) * own_rows]
            piece = jnp.concatenate([piece, jnp.zeros((pad_rows - own_rows, rows), jnp.float32)], axis=0)
            to = (zc * seq + t) * pad_rows
            x_t[who, to : to + pad_rows, :] = piece.astype(jnp.bfloat16)

    project(s)
    relays = []
    for k in range(2):
        x_copies[k, k].wait_recv()
        where = x_all.at[half_of(peers[k], k)]
        relays.append(send(where, where, r_ss.at[k], r_rs.at[k], (peers[1 - k], d)))
    transpose(s)
    for k in range(2):
        x_copies[k, 1 - k].wait_recv()
        project(peers[k])
    for k in range(2):
        transpose(peers[k])
    for k in range(2):
        relays[k].wait_recv()
    project(peers[2])
    transpose(peers[2])
    for copy in g_copies:
        copy.wait_recv()

    block = 256 if length % 256 == 0 else rows
    scale = hd ** (-0.5)
    dk_acc[...] = jnp.zeros_like(dk_acc)
    dv_acc[...] = jnp.zeros_like(dv_acc)
    d_own[:, 512:] = jnp.zeros((length, cw - 512), jnp.bfloat16)

    def attention(b, carry):
        at = pl.ds(pl.multiple_of(b * block, block), block)
        for h in range(2):
            q = qkv[at, h * LANES : (h + 1) * LANES]
            g = g_all[at, h * LANES : (h + 1) * LANES]
            keys = qkv[:, (2 + h) * LANES : (3 + h) * LANES]
            values = qkv[:, (4 + h) * LANES : (5 + h) * LANES]
            st = mm(keys, q, NT) * scale
            e = jnp.exp(st - jnp.max(st, axis=0, keepdims=True))
            p = e * (1.0 / jnp.sum(e, axis=0, keepdims=True))
            w = p.astype(jnp.bfloat16)
            dp = mm(values, g, NT)
            delta = jnp.sum(w.astype(jnp.float32) * dp, axis=0, keepdims=True)
            ds = (p * (dp - delta)).astype(jnp.bfloat16)
            dv_acc[h] += mm(w, g)
            dk_acc[h] += mm(ds, q)
            dq = mm(keys.T, ds).T * scale
            d_own[at, h * hd : (h + 1) * hd] = dq[:, :hd].astype(jnp.bfloat16)
        return carry

    lax.fori_loop(0, length // block, attention, 0)
    for h in range(2):
        at = pairw + h * hd
        d_own[:, at : at + hd] = (dk_acc[h, :, :hd] * scale).astype(jnp.bfloat16)
        at = 2 * pairw + h * hd
        d_own[:, at : at + hd] = dv_acc[h, :, :hd].astype(jnp.bfloat16)

    d_copies = [
        send(d_own.at[at_rows(p)], d_back.at[s], d_ss.at[k], d_rs.at[k], (p, d)) for k, p in enumerate(peers)
    ]
    d_back[s] = d_own[mine, :]

    span = seq * pad_rows
    core_copies, z_copies = [], []

    def pass_on(k):
        core_copies[k].wait_recv()
        p = zpeers[k]
        own = part[p, pl.ds(pl.multiple_of(c * span, 64), span), :].astype(jnp.float32)
        pair[k] = (own + core_in[p].astype(jnp.float32)).astype(jnp.bfloat16)
        z_copies.append(send(pair.at[k], z_in.at[k], z_ss.at[k], z_rs.at[k], (s, p * 2 + c)))

    for k, p in enumerate(zpeers + [z]):
        chunk = pl.ds(pl.multiple_of(p * (2 * span), 128), 2 * span)
        acc = mm(x_t[0, chunk, :], d_own[0:rows, :])
        for q in range(1, seq):
            acc = acc + mm(x_t[q, chunk, :], d_own[q * rows : (q + 1) * rows, :])
        part[p] = acc.astype(jnp.bfloat16)
        other = part.at[p, pl.ds(pl.multiple_of(oc * span, 64), span)]
        core_copies.append(send(other, core_in.at[p], c_ss.at[k], c_rs.at[k], (s, sib)))
        if k > 0:
            pass_on(k - 1)

    for copy in d_copies:
        copy.wait_recv()
    for p in range(seq):
        for i in range(3):
            at = i * attw + p * pairw
            d_cat[:, at : at + pairw] = d_back[p, :, i * pairw : (i + 1) * pairw]
    w_copies[3].wait()
    gt_out[...] = mm(d_cat[...], w_all[...]).astype(jnp.bfloat16)

    core_copies[-1].wait_recv()
    own = part[z, pl.ds(pl.multiple_of(c * span, 64), span), :].astype(jnp.float32)
    acc = own + core_in[z].astype(jnp.float32)
    for k in range(nz - 1):
        z_copies[k].wait_recv()
        acc = acc + z_in[k].astype(jnp.float32)
    acc = acc.astype(jnp.bfloat16)
    for t in range(seq):
        total[t] = acc[t * pad_rows : (t + 1) * pad_rows, :]
    f_copies = [send(total.at[p], last_in.at[s], f_ss.at[k], f_rs.at[k], (p, d)) for k, p in enumerate(peers)]
    last_in[s] = total[s]
    for copy in f_copies:
        copy.wait_recv()
    for p in range(seq):
        for i in range(3):
            at = i * attw + p * pairw
            gw_out[:, at : at + pairw] = last_in[p, :own_rows, i * pairw : (i + 1) * pairw].astype(jnp.float32)
    for copy in list(x_copies.values()) + relays + g_copies + d_copies + core_copies + z_copies + f_copies:
        copy.wait_send()


def fused(nz, tokens, qkv_weight, grad_out, keep):
    tokens, grad_out = tokens[0], grad_out[0]
    rows, width = tokens.shape
    cols = qkv_weight.shape[1]
    attw = cols // 3
    heads = attw // HEAD_DIM
    seq = heads // 2
    length = seq * rows
    own_rows = width // (seq * nz * 2)
    pad_rows = -(-own_rows // 16) * 16
    cw = -(-6 * HEAD_DIM // LANES) * LANES
    column = np.arange(width)
    freq = 10000.0 ** (-(2.0 * (column // 2)) / width) / (2.0 * np.pi)
    freq = jnp.asarray(freq[None, :].astype(np.float32))
    phase = jnp.asarray((0.25 * (column % 2))[None, :].astype(np.float32))
    bf16, f32 = jnp.bfloat16, jnp.float32
    vmem = pltpu.VMEM
    dma = pltpu.SemaphoreType.DMA
    scratch = [
        vmem((length, width), bf16),
        vmem((seq, rows, 2 * LANES), bf16),
        vmem((length, 2 * LANES), bf16),
        vmem((3, 2 * HEAD_DIM, width), bf16),
        vmem((cols, width), bf16),
        vmem((length, 6 * LANES), bf16),
        vmem((seq, 2 * nz * seq * pad_rows, rows), bf16),
        vmem((2, length, LANES), f32),
        vmem((2, length, LANES), f32),
        vmem((length, cw), bf16),
        vmem((seq, rows, cw), bf16),
        vmem((rows, cols), bf16),
        vmem((nz, 2 * seq * pad_rows, cw), bf16),
        vmem((nz, seq * pad_rows, cw), bf16),
        vmem((nz - 1, seq * pad_rows, cw), bf16),
        vmem((nz - 1, seq * pad_rows, cw), bf16),
        vmem((seq, pad_rows, cw), bf16),
        vmem((seq, pad_rows, cw), bf16),
        dma((4,)), dma((2, 2)), dma((2, 2)), dma((2,)), dma((2,)),
        dma((3,)), dma((3,)), dma((3,)), dma((3,)), dma((nz,)), dma((nz,)),
        dma((nz - 1,)), dma((nz - 1,)), dma((3,)), dma((3,)),
    ]
    whole = pl.BlockSpec(memory_space=pltpu.VMEM)
    gt, gw = pl.pallas_call(
        functools.partial(fused_kernel, nz, heads),
        out_shape=[
            jax.ShapeDtypeStruct((rows, width), bf16),
            jax.ShapeDtypeStruct((own_rows, cols), f32),
        ],
        in_specs=[whole, pl.BlockSpec(memory_space=pl.ANY)] + [whole] * 4,
        out_specs=[whole] * 2,
        scratch_shapes=scratch,
        compiler_params=pltpu.CompilerParams(
            collective_id=0, has_side_effects=True, vmem_limit_bytes=58 * 2**20
        ),
    )(tokens, qkv_weight.T, grad_out, keep, freq, phase)
    return gt[None], gw


def position_code(rowid, keep_row, width):
    visible = keep_row.shape[0]
    frame = rowid // visible
    slot = rowid % visible
    onehot = slot[:, None] == jnp.arange(visible, dtype=jnp.int32)[None, :]
    spatial = jnp.sum(jnp.where(onehot, keep_row[None, :], 0), axis=1)
    index = (frame * GRID + spatial).astype(jnp.float32)
    column = jnp.arange(width, dtype=jnp.int32)
    half = (column // 2).astype(jnp.float32)
    inverse = jnp.exp(-(2.0 * half / width) * jnp.log(10000.0))
    angle = index[:, None] * inverse[None, :]
    return jnp.where((column % 2 == 0)[None, :], jnp.sin(angle), jnp.cos(angle))


def attend(queries, keys, values, grads):
    length = queries.shape[0]
    scale = HEAD_DIM ** (-0.5)
    block = 512 if length % 512 == 0 else length
    count = length // block

    def step(carry, index):
        key_acc, value_acc = carry
        start = index * block
        q_block = lax.dynamic_slice_in_dim(queries, start, block, 0)
        g_block = lax.dynamic_slice_in_dim(grads, start, block, 0)
        scores = (
            jnp.einsum("qhd,khd->hqk", q_block, keys, preferred_element_type=jnp.float32) * scale
        )
        top = jnp.max(scores, axis=-1, keepdims=True)
        expo = jnp.exp(scores - top)
        probs = expo / jnp.sum(expo, axis=-1, keepdims=True)
        weights = probs.astype(jnp.bfloat16)
        attended = jnp.einsum("hqk,khd->qhd", weights, values, preferred_element_type=jnp.float32)
        delta = jnp.sum(g_block.astype(jnp.float32) * attended, axis=-1)
        dprobs = jnp.einsum("qhd,khd->hqk", g_block, values, preferred_element_type=jnp.float32)
        dscores = (probs * (dprobs - jnp.transpose(delta)[:, :, None])).astype(jnp.bfloat16)
        grad_q = (
            jnp.einsum("hqk,khd->qhd", dscores, keys, preferred_element_type=jnp.float32) * scale
        ).astype(jnp.bfloat16)
        key_acc = key_acc + jnp.einsum(
            "hqk,qhd->khd", dscores, q_block, preferred_element_type=jnp.float32
        )
        value_acc = value_acc + jnp.einsum(
            "hqk,qhd->khd", weights, g_block, preferred_element_type=jnp.float32
        )
        return ((key_acc, value_acc), grad_q)

    zeros = jnp.zeros(keys.shape, jnp.float32)
    (key_acc, value_acc), grad_blocks = lax.scan(
        step, (zeros, zeros), jnp.arange(count, dtype=jnp.int32)
    )
    grad_q = grad_blocks.reshape(queries.shape)
    grad_k = (key_acc * scale).astype(jnp.bfloat16)
    grad_v = value_acc.astype(jnp.bfloat16)
    return (grad_q, grad_k, grad_v)


def weight_term(inputs, grad_qkv):
    return lax.dot_general(
        inputs, grad_qkv, (((0,), (0,)), ((), ())), preferred_element_type=jnp.float32
    )


def local(tokens, qkv_weight, grad_out, keep):
    local_tokens = tokens[0]
    local_grads = grad_out[0]
    rows = local_tokens.shape[0]
    width = local_tokens.shape[1]
    attw = qkv_weight.shape[1] // 3
    rowid = lax.axis_index("seq") * rows + jnp.arange(rows, dtype=jnp.int32)
    code = position_code(rowid, keep[0], width)
    inputs = (local_tokens.astype(jnp.float32) + code).astype(jnp.bfloat16)
    qkv = jnp.dot(inputs, qkv_weight, preferred_element_type=jnp.float32).astype(jnp.bfloat16)
    head_q, head_k, head_v, head_g = (
        lax.all_to_all(qkv[:, :attw], "seq", split_axis=1, concat_axis=0, tiled=True),
        lax.all_to_all(qkv[:, attw : 2 * attw], "seq", split_axis=1, concat_axis=0, tiled=True),
        lax.all_to_all(qkv[:, 2 * attw :], "seq", split_axis=1, concat_axis=0, tiled=True),
        lax.all_to_all(local_grads, "seq", split_axis=1, concat_axis=0, tiled=True),
    )
    length = head_q.shape[0]
    narrow = head_q.shape[1]
    shape = (length, narrow // HEAD_DIM, HEAD_DIM)
    grad_q, grad_k, grad_v = attend(
        head_q.reshape(shape), head_k.reshape(shape), head_v.reshape(shape), head_g.reshape(shape)
    )
    flat_q = grad_q.reshape(length, narrow)
    flat_k = grad_k.reshape(length, narrow)
    flat_v = grad_v.reshape(length, narrow)
    back_q, back_k, back_v = (
        lax.all_to_all(flat_q, "seq", split_axis=0, concat_axis=1, tiled=True),
        lax.all_to_all(flat_k, "seq", split_axis=0, concat_axis=1, tiled=True),
        lax.all_to_all(flat_v, "seq", split_axis=0, concat_axis=1, tiled=True),
    )
    grad_qkv = jnp.concatenate([back_q, back_k, back_v], axis=1)
    grad_tokens = jnp.dot(
        grad_qkv, jnp.transpose(qkv_weight), preferred_element_type=jnp.float32
    ).astype(jnp.bfloat16)
    partial_rows = lax.psum_scatter(
        weight_term(inputs, grad_qkv).astype(jnp.bfloat16), "seq", scatter_dimension=0, tiled=True
    )
    grad_weight = lax.psum_scatter(partial_rows, "dp", scatter_dimension=0, tiled=True).astype(
        jnp.float32
    )
    return (grad_tokens[None], grad_weight)


def solution(mesh):
    in_specs = (P("dp", "seq", None), P(), P("dp", "seq", None), P("dp", None))
    out_specs = (P("dp", "seq", None), P(("seq", "dp"), None))
    seq, dp = mesh.shape["seq"], mesh.shape["dp"]

    def device(tokens, qkv_weight, grad_out, keep):
        heads = qkv_weight.shape[1] // 3 // HEAD_DIM
        rows = tokens.shape[1]
        if seq == 4 and heads == 2 * seq and dp % 2 == 0 and rows % 64 == 0:
            return fused(dp // 2, tokens, qkv_weight, grad_out, keep)
        return local(tokens, qkv_weight, grad_out, keep)

    return jax.shard_map(device, mesh=mesh, in_specs=in_specs, out_specs=out_specs, check_vma=False)
```

```python
import functools

import numpy as np
import jax
import jax.numpy as jnp
from jax import lax
from jax.experimental import pallas as pl
from jax.experimental.pallas import tpu as pltpu
from jax.sharding import PartitionSpec as P

HEAD_DIM = 88
GRID = 1024
MESH = pl.DeviceIdType.MESH
LANES = 128
SINE = (
    6.283182793407034,
    -41.34141938561695,
    81.59613875537907,
    -76.57968785099001,
    41.203743633541215,
    -12.268859940824616,
)
NT = (((1,), (1,)), ((), ()))
NN = (((1,), (0,)), ((), ()))


def mm(a, b, dims=NN):
    return lax.dot_general(a, b, dims, preferred_element_type=jnp.float32)


def fused_kernel(
    nz, heads, tokens, weight, grads, keep, freq, phase, gt_out, last_in,
    x_all, g_send, g_all, w_own, w_all, qkv, x_t, dk_acc, dv_acc, d_own, d_back, d_cat,
    part, core_in, pair, z_in, total,
    w_sem, x_ss, x_rs, r_ss, r_rs, g_ss, g_rs, d_ss, d_rs, c_ss, c_rs, z_ss, z_rs, f_ss, f_rs,
):
    hd = HEAD_DIM
    pairw = 2 * hd
    rows, width = tokens.shape
    attw = weight.shape[0] // 3
    seq = heads // 2
    length = seq * rows
    own_rows = width // (seq * nz * 2)
    pad_rows = total.shape[1]
    cw = d_own.shape[1]
    visible = keep.shape[1]
    s = lax.axis_index("seq")
    d = lax.axis_index("dp")
    z = d // 2
    c = d % 2
    oc = 1 - c
    sib = z * 2 + oc
    peers = (s + 1 - 2 * (s % 2), (s + 2) % 4, 3 - s)
    zpeers = [(z + k) % nz for k in range(1, nz)]
    zsrcs = [(z + nz - k) % nz for k in range(1, nz)]

    def at_rows(who):
        return pl.ds(pl.multiple_of(who * rows, 64), rows)

    def send(src, dst, ss, rs, dev):
        copy = pltpu.make_async_remote_copy(
            src_ref=src, dst_ref=dst, send_sem=ss, recv_sem=rs,
            device_id=dev, device_id_type=MESH,
        )
        copy.start()
        return copy

    w_copies = [
        pltpu.make_async_copy(
            weight.at[pl.ds(pl.multiple_of(i * attw + s * pairw, 16), pairw)], w_own.at[i], w_sem.at[i]
        )
        for i in range(3)
    ]
    w_copies.append(pltpu.make_async_copy(weight, w_all, w_sem.at[3]))
    for copy in w_copies:
        copy.start()

    barrier = pltpu.get_barrier_semaphore()
    for p in peers:
        pl.semaphore_signal(barrier, inc=1, device_id=(p, d), device_id_type=MESH)
    pl.semaphore_signal(barrier, inc=1, device_id=(s, sib), device_id_type=MESH)
    for p in zpeers:
        pl.semaphore_signal(barrier, inc=1, device_id=(s, p * 2 + c), device_id_type=MESH)

    row = s * rows + lax.broadcasted_iota(jnp.int32, (rows, visible), 0)
    frame = row // visible
    slot = row - frame * visible
    lane = lax.broadcasted_iota(jnp.int32, (rows, visible), 1)
    spot = jnp.where(slot == lane, (frame * GRID + keep[...]).astype(jnp.float32), 0.0)
    index = jnp.sum(spot, axis=1, keepdims=True)
    mine = at_rows(s)
    half = rows // 2

    def half_of(who, i):
        return pl.ds(pl.multiple_of(who * rows + i * half, 32), half)

    for i in range(2):
        lo = i * half
        turns = index[lo : lo + half] * freq[...] + phase[...]
        r = turns - jnp.floor(turns + 0.5)
        r2 = r * r
        poly = jnp.full_like(r2, SINE[-1])
        for coef in SINE[-2::-1]:
            poly = poly * r2 + coef
        x = (tokens[lo : lo + half, :].astype(jnp.float32) + poly * r).astype(jnp.bfloat16)
        x_all[half_of(s, i), :] = x
    pl.semaphore_wait(barrier, 4 + nz - 1)
    x_copies = {}
    for k, i in ((0, 0), (1, 1), (0, 1), (1, 0)):
        where = x_all.at[half_of(s, i)]
        x_copies[k, i] = send(where, where, x_ss.at[k, i], x_rs.at[k, i], (peers[k], d))

    g_send[...] = jnp.zeros_like(g_send)
    for p in range(seq):
        for h in range(2):
            g_send[p, :, h * LANES : h * LANES + hd] = grads[:, p * pairw + h * hd : p * pairw + (h + 1) * hd]
    g_all[mine, :] = g_send[s]

    qkv[...] = jnp.zeros_like(qkv)
    for copy in w_copies[:3]:
        copy.wait()

    def project(who):
        x = x_all[at_rows(who), :]
        for i in range(3):
            out = mm(x, w_own[i], NT).astype(jnp.bfloat16)
            for h in range(2):
                to = (2 * i + h) * LANES
                qkv[at_rows(who), to : to + hd] = out[:, h * hd : (h + 1) * hd]

    def transpose(who):
        xt = x_all[at_rows(who), :].astype(jnp.float32).T
        for r in range(width // own_rows):
            t, zc = r // (2 * nz), r % (2 * nz)
            piece = xt[r * own_rows : (r + 1) * own_rows]
            piece = jnp.concatenate([piece, jnp.zeros((pad_rows - own_rows, rows), jnp.float32)], axis=0)
            to = (zc * seq + t) * pad_rows
            x_t[who, to : to + pad_rows, :] = piece.astype(jnp.bfloat16)

    project(s)
    relays = []
    for k in range(2):
        x_copies[k, k].wait_recv()
        where = x_all.at[half_of(peers[k], k)]
        relays.append(send(where, where, r_ss.at[k], r_rs.at[k], (peers[1 - k], d)))
    g_copies = [
        send(g_send.at[p], g_all.at[mine], g_ss.at[k], g_rs.at[k], (p, d)) for k, p in enumerate(peers)
    ]
    transpose(s)
    for k in range(2):
        x_copies[k, 1 - k].wait_recv()
        project(peers[k])
    for k in range(2):
        transpose(peers[k])
    for k in range(2):
        relays[k].wait_recv()
    project(peers[2])
    transpose(peers[2])
    for copy in g_copies:
        copy.wait_recv()

    block = 256 if length % 256 == 0 else rows
    scale = hd ** (-0.5)
    dk_acc[...] = jnp.zeros_like(dk_acc)
    dv_acc[...] = jnp.zeros_like(dv_acc)
    d_own[:, 512:] = jnp.zeros((length, cw - 512), jnp.bfloat16)

    def attention(b, carry):
        at = pl.ds(pl.multiple_of(b * block, block), block)
        for h in range(2):
            q = qkv[at, h * LANES : (h + 1) * LANES]
            g = g_all[at, h * LANES : (h + 1) * LANES]
            keys = qkv[:, (2 + h) * LANES : (3 + h) * LANES]
            values = qkv[:, (4 + h) * LANES : (5 + h) * LANES]
            st = mm(keys, q, NT) * scale
            e = jnp.exp(st - jnp.max(st, axis=0, keepdims=True))
            p = e * (1.0 / jnp.sum(e, axis=0, keepdims=True))
            w = p.astype(jnp.bfloat16)
            dp = mm(values, g, NT)
            delta = jnp.sum(w.astype(jnp.float32) * dp, axis=0, keepdims=True)
            ds = (p * (dp - delta)).astype(jnp.bfloat16)
            dv_acc[h] += mm(w, g)
            dk_acc[h] += mm(ds, q)
            dq = mm(keys.T, ds).T * scale
            d_own[at, h * hd : (h + 1) * hd] = dq[:, :hd].astype(jnp.bfloat16)
        return carry

    lax.fori_loop(0, length // block, attention, 0)
    for h in range(2):
        at = pairw + h * hd
        d_own[:, at : at + hd] = (dk_acc[h, :, :hd] * scale).astype(jnp.bfloat16)
        at = 2 * pairw + h * hd
        d_own[:, at : at + hd] = dv_acc[h, :, :hd].astype(jnp.bfloat16)

    d_copies = [
        send(d_own.at[at_rows(p)], d_back.at[s], d_ss.at[k], d_rs.at[k], (p, d)) for k, p in enumerate(peers)
    ]
    d_back[s] = d_own[mine, :]

    span = seq * pad_rows
    core_copies, z_copies = [], []

    def pass_on(k):
        core_copies[k].wait_recv()
        p = zpeers[k]
        own = part[p, pl.ds(pl.multiple_of(c * span, 64), span), :].astype(jnp.float32)
        pair[k] = (own + core_in[p].astype(jnp.float32)).astype(jnp.bfloat16)
        z_copies.append(send(pair.at[k], z_in.at[k], z_ss.at[k], z_rs.at[k], (s, p * 2 + c)))

    for k, p in enumerate(zpeers + [z]):
        chunk = pl.ds(pl.multiple_of(p * (2 * span), 128), 2 * span)
        acc = mm(x_t[0, chunk, :], d_own[0:rows, :])
        for q in range(1, seq):
            acc = acc + mm(x_t[q, chunk, :], d_own[q * rows : (q + 1) * rows, :])
        part[p] = acc.astype(jnp.bfloat16)
        other = part.at[p, pl.ds(pl.multiple_of(oc * span, 64), span)]
        core_copies.append(send(other, core_in.at[p], c_ss.at[k], c_rs.at[k], (s, sib)))
        if k > 0:
            pass_on(k - 1)

    for copy in d_copies:
        copy.wait_recv()
    for p in range(seq):
        for i in range(3):
            at = i * attw + p * pairw
            d_cat[:, at : at + pairw] = d_back[p, :, i * pairw : (i + 1) * pairw]
    w_copies[3].wait()
    gt_out[...] = mm(d_cat[...], w_all[...]).astype(jnp.bfloat16)

    core_copies[-1].wait_recv()
    own = part[z, pl.ds(pl.multiple_of(c * span, 64), span), :].astype(jnp.float32)
    acc = own + core_in[z].astype(jnp.float32)
    for k in range(nz - 1):
        z_copies[k].wait_recv()
        acc = acc + z_in[k].astype(jnp.float32)
    acc = acc.astype(jnp.bfloat16)
    for t in range(seq):
        total[t] = acc[t * pad_rows : (t + 1) * pad_rows, :]
    f_copies = [send(total.at[p], last_in.at[s], f_ss.at[k], f_rs.at[k], (p, d)) for k, p in enumerate(peers)]
    last_in[s] = total[s]
    for copy in f_copies:
        copy.wait_recv()
    for copy in list(x_copies.values()) + relays + g_copies + d_copies + core_copies + z_copies + f_copies:
        copy.wait_send()


def finish_kernel(last_in, gt_in, gt_out, gw_out, sem):
    copy = pltpu.make_async_copy(gt_in, gt_out, sem)
    copy.start()
    seq = last_in.shape[0]
    pairw = 2 * HEAD_DIM
    attw = gw_out.shape[1] // 3
    for p in range(seq):
        for i in range(3):
            at = i * attw + p * pairw
            piece = last_in[p, : gw_out.shape[0], i * pairw : (i + 1) * pairw]
            gw_out[:, at : at + pairw] = piece.astype(jnp.float32)
    copy.wait()


def fused(nz, tokens, qkv_weight, grad_out, keep):
    tokens, grad_out = tokens[0], grad_out[0]
    rows, width = tokens.shape
    cols = qkv_weight.shape[1]
    attw = cols // 3
    heads = attw // HEAD_DIM
    seq = heads // 2
    length = seq * rows
    own_rows = width // (seq * nz * 2)
    pad_rows = -(-own_rows // 16) * 16
    cw = -(-6 * HEAD_DIM // LANES) * LANES
    column = np.arange(width)
    freq = 10000.0 ** (-(2.0 * (column // 2)) / width) / (2.0 * np.pi)
    freq = jnp.asarray(freq[None, :].astype(np.float32))
    phase = jnp.asarray((0.25 * (column % 2))[None, :].astype(np.float32))
    bf16, f32 = jnp.bfloat16, jnp.float32
    vmem = pltpu.VMEM
    dma = pltpu.SemaphoreType.DMA
    scratch = [
        vmem((length, width), bf16),
        vmem((seq, rows, 2 * LANES), bf16),
        vmem((length, 2 * LANES), bf16),
        vmem((3, 2 * HEAD_DIM, width), bf16),
        vmem((cols, width), bf16),
        vmem((length, 6 * LANES), bf16),
        vmem((seq, 2 * nz * seq * pad_rows, rows), bf16),
        vmem((2, length, LANES), f32),
        vmem((2, length, LANES), f32),
        vmem((length, cw), bf16),
        vmem((seq, rows, cw), bf16),
        vmem((rows, cols), bf16),
        vmem((nz, 2 * seq * pad_rows, cw), bf16),
        vmem((nz, seq * pad_rows, cw), bf16),
        vmem((nz - 1, seq * pad_rows, cw), bf16),
        vmem((nz - 1, seq * pad_rows, cw), bf16),
        vmem((seq, pad_rows, cw), bf16),
        dma((4,)), dma((2, 2)), dma((2, 2)), dma((2,)), dma((2,)),
        dma((3,)), dma((3,)), dma((3,)), dma((3,)), dma((nz,)), dma((nz,)),
        dma((nz - 1,)), dma((nz - 1,)), dma((3,)), dma((3,)),
    ]
    whole = pl.BlockSpec(memory_space=pltpu.VMEM)
    gt, last = pl.pallas_call(
        functools.partial(fused_kernel, nz, heads),
        out_shape=[
            jax.ShapeDtypeStruct((rows, width), bf16),
            jax.ShapeDtypeStruct((seq, pad_rows, cw), bf16),
        ],
        in_specs=[whole, pl.BlockSpec(memory_space=pl.ANY)] + [whole] * 4,
        out_specs=[whole] * 2,
        scratch_shapes=scratch,
        compiler_params=pltpu.CompilerParams(
            collective_id=0, has_side_effects=True, vmem_limit_bytes=58 * 2**20
        ),
    )(tokens, qkv_weight.T, grad_out, keep, freq, phase)
    anywhere = pl.BlockSpec(memory_space=pl.ANY)
    gt, gw = pl.pallas_call(
        finish_kernel,
        out_shape=[
            jax.ShapeDtypeStruct((rows, width), bf16),
            jax.ShapeDtypeStruct((own_rows, cols), f32),
        ],
        in_specs=[whole, anywhere],
        out_specs=[anywhere, whole],
        scratch_shapes=[dma],
    )(last, gt)
    return gt[None], gw


def position_code(rowid, keep_row, width):
    visible = keep_row.shape[0]
    frame = rowid // visible
    slot = rowid % visible
    onehot = slot[:, None] == jnp.arange(visible, dtype=jnp.int32)[None, :]
    spatial = jnp.sum(jnp.where(onehot, keep_row[None, :], 0), axis=1)
    index = (frame * GRID + spatial).astype(jnp.float32)
    column = jnp.arange(width, dtype=jnp.int32)
    half = (column // 2).astype(jnp.float32)
    inverse = jnp.exp(-(2.0 * half / width) * jnp.log(10000.0))
    angle = index[:, None] * inverse[None, :]
    return jnp.where((column % 2 == 0)[None, :], jnp.sin(angle), jnp.cos(angle))


def attend(queries, keys, values, grads):
    length = queries.shape[0]
    scale = HEAD_DIM ** (-0.5)
    block = 512 if length % 512 == 0 else length
    count = length // block

    def step(carry, index):
        key_acc, value_acc = carry
        start = index * block
        q_block = lax.dynamic_slice_in_dim(queries, start, block, 0)
        g_block = lax.dynamic_slice_in_dim(grads, start, block, 0)
        scores = (
            jnp.einsum("qhd,khd->hqk", q_block, keys, preferred_element_type=jnp.float32) * scale
        )
        top = jnp.max(scores, axis=-1, keepdims=True)
        expo = jnp.exp(scores - top)
        probs = expo / jnp.sum(expo, axis=-1, keepdims=True)
        weights = probs.astype(jnp.bfloat16)
        attended = jnp.einsum("hqk,khd->qhd", weights, values, preferred_element_type=jnp.float32)
        delta = jnp.sum(g_block.astype(jnp.float32) * attended, axis=-1)
        dprobs = jnp.einsum("qhd,khd->hqk", g_block, values, preferred_element_type=jnp.float32)
        dscores = (probs * (dprobs - jnp.transpose(delta)[:, :, None])).astype(jnp.bfloat16)
        grad_q = (
            jnp.einsum("hqk,khd->qhd", dscores, keys, preferred_element_type=jnp.float32) * scale
        ).astype(jnp.bfloat16)
        key_acc = key_acc + jnp.einsum(
            "hqk,qhd->khd", dscores, q_block, preferred_element_type=jnp.float32
        )
        value_acc = value_acc + jnp.einsum(
            "hqk,qhd->khd", weights, g_block, preferred_element_type=jnp.float32
        )
        return ((key_acc, value_acc), grad_q)

    zeros = jnp.zeros(keys.shape, jnp.float32)
    (key_acc, value_acc), grad_blocks = lax.scan(
        step, (zeros, zeros), jnp.arange(count, dtype=jnp.int32)
    )
    grad_q = grad_blocks.reshape(queries.shape)
    grad_k = (key_acc * scale).astype(jnp.bfloat16)
    grad_v = value_acc.astype(jnp.bfloat16)
    return (grad_q, grad_k, grad_v)


def weight_term(inputs, grad_qkv):
    return lax.dot_general(
        inputs, grad_qkv, (((0,), (0,)), ((), ())), preferred_element_type=jnp.float32
    )


def local(tokens, qkv_weight, grad_out, keep):
    local_tokens = tokens[0]
    local_grads = grad_out[0]
    rows = local_tokens.shape[0]
    width = local_tokens.shape[1]
    attw = qkv_weight.shape[1] // 3
    rowid = lax.axis_index("seq") * rows + jnp.arange(rows, dtype=jnp.int32)
    code = position_code(rowid, keep[0], width)
    inputs = (local_tokens.astype(jnp.float32) + code).astype(jnp.bfloat16)
    qkv = jnp.dot(inputs, qkv_weight, preferred_element_type=jnp.float32).astype(jnp.bfloat16)
    head_q, head_k, head_v, head_g = (
        lax.all_to_all(qkv[:, :attw], "seq", split_axis=1, concat_axis=0, tiled=True),
        lax.all_to_all(qkv[:, attw : 2 * attw], "seq", split_axis=1, concat_axis=0, tiled=True),
        lax.all_to_all(qkv[:, 2 * attw :], "seq", split_axis=1, concat_axis=0, tiled=True),
        lax.all_to_all(local_grads, "seq", split_axis=1, concat_axis=0, tiled=True),
    )
    length = head_q.shape[0]
    narrow = head_q.shape[1]
    shape = (length, narrow // HEAD_DIM, HEAD_DIM)
    grad_q, grad_k, grad_v = attend(
        head_q.reshape(shape), head_k.reshape(shape), head_v.reshape(shape), head_g.reshape(shape)
    )
    flat_q = grad_q.reshape(length, narrow)
    flat_k = grad_k.reshape(length, narrow)
    flat_v = grad_v.reshape(length, narrow)
    back_q, back_k, back_v = (
        lax.all_to_all(flat_q, "seq", split_axis=0, concat_axis=1, tiled=True),
        lax.all_to_all(flat_k, "seq", split_axis=0, concat_axis=1, tiled=True),
        lax.all_to_all(flat_v, "seq", split_axis=0, concat_axis=1, tiled=True),
    )
    grad_qkv = jnp.concatenate([back_q, back_k, back_v], axis=1)
    grad_tokens = jnp.dot(
        grad_qkv, jnp.transpose(qkv_weight), preferred_element_type=jnp.float32
    ).astype(jnp.bfloat16)
    partial_rows = lax.psum_scatter(
        weight_term(inputs, grad_qkv).astype(jnp.bfloat16), "seq", scatter_dimension=0, tiled=True
    )
    grad_weight = lax.psum_scatter(partial_rows, "dp", scatter_dimension=0, tiled=True).astype(
        jnp.float32
    )
    return (grad_tokens[None], grad_weight)


def solution(mesh):
    in_specs = (P("dp", "seq", None), P(), P("dp", "seq", None), P("dp", None))
    out_specs = (P("dp", "seq", None), P(("seq", "dp"), None))
    seq, dp = mesh.shape["seq"], mesh.shape["dp"]

    def device(tokens, qkv_weight, grad_out, keep):
        heads = qkv_weight.shape[1] // 3 // HEAD_DIM
        rows = tokens.shape[1]
        if seq == 4 and heads == 2 * seq and dp % 2 == 0 and rows % 64 == 0:
            return fused(dp // 2, tokens, qkv_weight, grad_out, keep)
        return local(tokens, qkv_weight, grad_out, keep)

    return jax.shard_map(device, mesh=mesh, in_specs=in_specs, out_specs=out_specs, check_vma=False)
```

```python
import functools

import numpy as np
import jax
import jax.numpy as jnp
from jax import lax
from jax.experimental import pallas as pl
from jax.experimental.pallas import tpu as pltpu
from jax.sharding import PartitionSpec as P

HEAD_DIM = 88
GRID = 1024
MESH = pl.DeviceIdType.MESH
LANES = 128
SINE = (
    6.283182793407034,
    -41.34141938561695,
    81.59613875537907,
    -76.57968785099001,
    41.203743633541215,
    -12.268859940824616,
)
NT = (((1,), (1,)), ((), ()))
NN = (((1,), (0,)), ((), ()))


def mm(a, b, dims=NN):
    return lax.dot_general(a, b, dims, preferred_element_type=jnp.float32)


def fused_kernel(
    nz, heads, tokens, weight, grads, keep, freq, phase, gt_out, last_in,
    x_all, g_send, g_all, w_own, w_all, qkv, x_t, dk_acc, dv_acc, d_own, d_back, d_cat,
    part, core_in, pair, z_in, run, total,
    w_sem, x_ss, x_rs, r_ss, r_rs, g_ss, g_rs, d_ss, d_rs, c_ss, c_rs, z_ss, z_rs, f_ss, f_rs,
):
    hd = HEAD_DIM
    pairw = 2 * hd
    rows, width = tokens.shape
    attw = weight.shape[0] // 3
    seq = heads // 2
    length = seq * rows
    own_rows = width // (seq * nz * 2)
    pad_rows = total.shape[1]
    cw = d_own.shape[1]
    visible = keep.shape[1]
    s = lax.axis_index("seq")
    d = lax.axis_index("dp")
    z = d // 2
    c = d % 2
    oc = 1 - c
    sib = z * 2 + oc
    peers = (s + 1 - 2 * (s % 2), (s + 2) % 4, 3 - s)
    zpeers = [(z + k) % nz for k in range(1, nz)]
    zsrcs = [(z + nz - k) % nz for k in range(1, nz)]

    def at_rows(who):
        return pl.ds(pl.multiple_of(who * rows, 64), rows)

    def send(src, dst, ss, rs, dev):
        copy = pltpu.make_async_remote_copy(
            src_ref=src, dst_ref=dst, send_sem=ss, recv_sem=rs,
            device_id=dev, device_id_type=MESH,
        )
        copy.start()
        return copy

    w_copies = [
        pltpu.make_async_copy(
            weight.at[pl.ds(pl.multiple_of(i * attw + s * pairw, 16), pairw)], w_own.at[i], w_sem.at[i]
        )
        for i in range(3)
    ]
    w_copies.append(pltpu.make_async_copy(weight, w_all, w_sem.at[3]))
    for copy in w_copies:
        copy.start()

    barrier = pltpu.get_barrier_semaphore()
    for p in peers:
        pl.semaphore_signal(barrier, inc=1, device_id=(p, d), device_id_type=MESH)
    pl.semaphore_signal(barrier, inc=1, device_id=(s, sib), device_id_type=MESH)
    for p in zpeers:
        pl.semaphore_signal(barrier, inc=1, device_id=(s, p * 2 + c), device_id_type=MESH)

    row = s * rows + lax.broadcasted_iota(jnp.int32, (rows, visible), 0)
    frame = row // visible
    slot = row - frame * visible
    lane = lax.broadcasted_iota(jnp.int32, (rows, visible), 1)
    spot = jnp.where(slot == lane, (frame * GRID + keep[...]).astype(jnp.float32), 0.0)
    index = jnp.sum(spot, axis=1, keepdims=True)
    mine = at_rows(s)
    half = rows // 2

    def half_of(who, i):
        return pl.ds(pl.multiple_of(who * rows + i * half, 32), half)

    for i in range(2):
        lo = i * half
        turns = index[lo : lo + half] * freq[...] + phase[...]
        r = turns - jnp.floor(turns + 0.5)
        r2 = r * r
        poly = jnp.full_like(r2, SINE[-1])
        for coef in SINE[-2::-1]:
            poly = poly * r2 + coef
        x = (tokens[lo : lo + half, :].astype(jnp.float32) + poly * r).astype(jnp.bfloat16)
        x_all[half_of(s, i), :] = x
    pl.semaphore_wait(barrier, 4 + nz - 1)
    x_copies = {}
    for k, i in ((0, 0), (1, 1), (0, 1), (1, 0)):
        where = x_all.at[half_of(s, i)]
        x_copies[k, i] = send(where, where, x_ss.at[k, i], x_rs.at[k, i], (peers[k], d))

    g_send[...] = jnp.zeros_like(g_send)
    for p in range(seq):
        for h in range(2):
            g_send[p, :, h * LANES : h * LANES + hd] = grads[:, p * pairw + h * hd : p * pairw + (h + 1) * hd]
    g_all[mine, :] = g_send[s]

    qkv[...] = jnp.zeros_like(qkv)
    for copy in w_copies[:3]:
        copy.wait()

    def project(who):
        x = x_all[at_rows(who), :]
        for i in range(3):
            out = mm(x, w_own[i], NT).astype(jnp.bfloat16)
            for h in range(2):
                to = (2 * i + h) * LANES
                qkv[at_rows(who), to : to + hd] = out[:, h * hd : (h + 1) * hd]

    def transpose(who):
        xt = x_all[at_rows(who), :].astype(jnp.float32).T
        for r in range(width // own_rows):
            t, zc = r // (2 * nz), r % (2 * nz)
            piece = xt[r * own_rows : (r + 1) * own_rows]
            piece = jnp.concatenate([piece, jnp.zeros((pad_rows - own_rows, rows), jnp.float32)], axis=0)
            to = (zc * seq + t) * pad_rows
            x_t[who, to : to + pad_rows, :] = piece.astype(jnp.bfloat16)

    project(s)
    relays = []
    for k in range(2):
        x_copies[k, k].wait_recv()
        where = x_all.at[half_of(peers[k], k)]
        relays.append(send(where, where, r_ss.at[k], r_rs.at[k], (peers[1 - k], d)))
    g_copies = [
        send(g_send.at[p], g_all.at[mine], g_ss.at[k], g_rs.at[k], (p, d)) for k, p in enumerate(peers)
    ]
    transpose(s)
    for k in range(2):
        x_copies[k, 1 - k].wait_recv()
        project(peers[k])
    for k in range(2):
        transpose(peers[k])
    for k in range(2):
        relays[k].wait_recv()
    project(peers[2])
    transpose(peers[2])
    for copy in g_copies:
        copy.wait_recv()

    block = 256 if length % 256 == 0 else rows
    scale = hd ** (-0.5)
    dk_acc[...] = jnp.zeros_like(dk_acc)
    dv_acc[...] = jnp.zeros_like(dv_acc)
    d_own[:, 512:] = jnp.zeros((length, cw - 512), jnp.bfloat16)

    def attention(b, carry):
        at = pl.ds(pl.multiple_of(b * block, block), block)
        for h in range(2):
            q = qkv[at, h * LANES : (h + 1) * LANES]
            g = g_all[at, h * LANES : (h + 1) * LANES]
            keys = qkv[:, (2 + h) * LANES : (3 + h) * LANES]
            values = qkv[:, (4 + h) * LANES : (5 + h) * LANES]
            st = mm(keys, q, NT) * scale
            e = jnp.exp(st - jnp.max(st, axis=0, keepdims=True))
            p = e * (1.0 / jnp.sum(e, axis=0, keepdims=True))
            w = p.astype(jnp.bfloat16)
            dp = mm(values, g, NT)
            delta = jnp.sum(w.astype(jnp.float32) * dp, axis=0, keepdims=True)
            ds = (p * (dp - delta)).astype(jnp.bfloat16)
            dv_acc[h] += mm(w, g)
            dk_acc[h] += mm(ds, q)
            dq = mm(keys.T, ds).T * scale
            d_own[at, h * hd : (h + 1) * hd] = dq[:, :hd].astype(jnp.bfloat16)
        return carry

    lax.fori_loop(0, length // block, attention, 0)
    for h in range(2):
        at = pairw + h * hd
        d_own[:, at : at + hd] = (dk_acc[h, :, :hd] * scale).astype(jnp.bfloat16)
        at = 2 * pairw + h * hd
        d_own[:, at : at + hd] = dv_acc[h, :, :hd].astype(jnp.bfloat16)

    d_copies = [
        send(d_own.at[at_rows(p)], d_back.at[s], d_ss.at[k], d_rs.at[k], (p, d)) for k, p in enumerate(peers)
    ]
    d_back[s] = d_own[mine, :]

    span = seq * pad_rows
    core_copies = []
    flip = z // (nz // 2)
    zm = z + flip * (nz - 1 - 2 * z)
    order = [p for k in range(nz // 2) for p in (nz - 1 - k, k)]

    def own_part(p):
        mine_part = part[p, pl.ds(pl.multiple_of(c * span, 64), span), :].astype(jnp.float32)
        return mine_part + core_in[p].astype(jnp.float32)

    def hop(p, way, to):
        return pltpu.make_async_remote_copy(
            src_ref=pair.at[p], dst_ref=z_in.at[way, p], send_sem=z_ss.at[p], recv_sem=z_rs.at[way, p],
            device_id=(s, to * 2 + c), device_id_type=MESH,
        )

    def pass_on(k):
        core_copies[k].wait_recv()
        p0 = order[k]
        p = p0 + flip * (nz - 1 - 2 * p0)

        @pl.when(p0 > zm)
        def _():
            onward = hop(p, flip, z + 1 - 2 * flip)
            run[...] = own_part(p)

            @pl.when(zm > 0)
            def _():
                onward.wait_recv()
                run[...] += z_in[flip, p].astype(jnp.float32)

            pair[p] = run[...].astype(jnp.bfloat16)
            onward.start()

        @pl.when(p0 < zm)
        def _():
            back = hop(p, 1 - flip, z - 1 + 2 * flip)
            back.wait_recv()
            pair[p] = (own_part(p) + z_in[1 - flip, p].astype(jnp.float32)).astype(jnp.bfloat16)
            back.start()

    for k, p0 in enumerate(order):
        p = p0 + flip * (nz - 1 - 2 * p0)
        chunk = pl.ds(pl.multiple_of(p * (2 * span), 128), 2 * span)
        acc = mm(x_t[0, chunk, :], d_own[0:rows, :])
        for q in range(1, seq):
            acc = acc + mm(x_t[q, chunk, :], d_own[q * rows : (q + 1) * rows, :])
        part[p] = acc.astype(jnp.bfloat16)
        other = part.at[p, pl.ds(pl.multiple_of(oc * span, 64), span)]
        core_copies.append(send(other, core_in.at[p], c_ss.at[k], c_rs.at[k], (s, sib)))
        if k > 0:
            pass_on(k - 1)
    pass_on(nz - 1)

    for copy in d_copies:
        copy.wait_recv()
    for p in range(seq):
        for i in range(3):
            at = i * attw + p * pairw
            d_cat[:, at : at + pairw] = d_back[p, :, i * pairw : (i + 1) * pairw]
    w_copies[3].wait()
    gt_out[...] = mm(d_cat[...], w_all[...]).astype(jnp.bfloat16)

    run[...] = own_part(z)

    @pl.when(z > 0)
    def _():
        hop(z, 0, (z + 1) % nz).wait_recv()
        run[...] += z_in[0, z].astype(jnp.float32)

    @pl.when(z < nz - 1)
    def _():
        hop(z, 1, (z + 1) % nz).wait_recv()
        run[...] += z_in[1, z].astype(jnp.float32)

    acc = run[...]
    acc = acc.astype(jnp.bfloat16)
    for t in range(seq):
        total[t] = acc[t * pad_rows : (t + 1) * pad_rows, :]
    f_copies = [send(total.at[p], last_in.at[s], f_ss.at[k], f_rs.at[k], (p, d)) for k, p in enumerate(peers)]
    last_in[s] = total[s]
    for copy in f_copies:
        copy.wait_recv()
    for copy in list(x_copies.values()) + relays + g_copies + d_copies + core_copies + f_copies:
        copy.wait_send()
    for p in zpeers:
        hop(p, 0, p).wait_send()


def finish_kernel(last_in, gt_in, gt_out, gw_out):
    gt_out[...] = gt_in[...]
    seq = last_in.shape[0]
    pairw = 2 * HEAD_DIM
    attw = gw_out.shape[1] // 3
    for p in range(seq):
        for i in range(3):
            at = i * attw + p * pairw
            piece = last_in[p, : gw_out.shape[0], i * pairw : (i + 1) * pairw]
            gw_out[:, at : at + pairw] = piece.astype(jnp.float32)


def fused(nz, tokens, qkv_weight, grad_out, keep):
    tokens, grad_out = tokens[0], grad_out[0]
    rows, width = tokens.shape
    cols = qkv_weight.shape[1]
    attw = cols // 3
    heads = attw // HEAD_DIM
    seq = heads // 2
    length = seq * rows
    own_rows = width // (seq * nz * 2)
    pad_rows = -(-own_rows // 16) * 16
    cw = -(-6 * HEAD_DIM // LANES) * LANES
    column = np.arange(width)
    freq = 10000.0 ** (-(2.0 * (column // 2)) / width) / (2.0 * np.pi)
    freq = jnp.asarray(freq[None, :].astype(np.float32))
    phase = jnp.asarray((0.25 * (column % 2))[None, :].astype(np.float32))
    bf16, f32 = jnp.bfloat16, jnp.float32
    vmem = pltpu.VMEM
    dma = pltpu.SemaphoreType.DMA
    scratch = [
        vmem((length, width), bf16),
        vmem((seq, rows, 2 * LANES), bf16),
        vmem((length, 2 * LANES), bf16),
        vmem((3, 2 * HEAD_DIM, width), bf16),
        vmem((cols, width), bf16),
        vmem((length, 6 * LANES), bf16),
        vmem((seq, 2 * nz * seq * pad_rows, rows), bf16),
        vmem((2, length, LANES), f32),
        vmem((2, length, LANES), f32),
        vmem((length, cw), bf16),
        vmem((seq, rows, cw), bf16),
        vmem((rows, cols), bf16),
        vmem((nz, 2 * seq * pad_rows, cw), bf16),
        vmem((nz, seq * pad_rows, cw), bf16),
        vmem((nz, seq * pad_rows, cw), bf16),
        vmem((2, nz, seq * pad_rows, cw), bf16),
        vmem((seq * pad_rows, cw), f32),
        vmem((seq, pad_rows, cw), bf16),
        dma((4,)), dma((2, 2)), dma((2, 2)), dma((2,)), dma((2,)),
        dma((3,)), dma((3,)), dma((3,)), dma((3,)), dma((nz,)), dma((nz,)),
        dma((nz,)), dma((2, nz)), dma((3,)), dma((3,)),
    ]
    whole = pl.BlockSpec(memory_space=pltpu.VMEM)
    gt, last = pl.pallas_call(
        functools.partial(fused_kernel, nz, heads),
        out_shape=[
            jax.ShapeDtypeStruct((rows, width), bf16),
            jax.ShapeDtypeStruct((seq, pad_rows, cw), bf16),
        ],
        in_specs=[whole, pl.BlockSpec(memory_space=pl.ANY)] + [whole] * 4,
        out_specs=[whole] * 2,
        scratch_shapes=scratch,
        compiler_params=pltpu.CompilerParams(
            collective_id=0, has_side_effects=True, vmem_limit_bytes=58 * 2**20
        ),
    )(tokens, qkv_weight.T, grad_out, keep, freq, phase)
    gt, gw = pl.pallas_call(
        finish_kernel,
        out_shape=[
            jax.ShapeDtypeStruct((rows, width), bf16),
            jax.ShapeDtypeStruct((own_rows, cols), f32),
        ],
        in_specs=[whole] * 2,
        out_specs=[whole] * 2,
    )(last, gt)
    return gt[None], gw


def position_code(rowid, keep_row, width):
    visible = keep_row.shape[0]
    frame = rowid // visible
    slot = rowid % visible
    onehot = slot[:, None] == jnp.arange(visible, dtype=jnp.int32)[None, :]
    spatial = jnp.sum(jnp.where(onehot, keep_row[None, :], 0), axis=1)
    index = (frame * GRID + spatial).astype(jnp.float32)
    column = jnp.arange(width, dtype=jnp.int32)
    half = (column // 2).astype(jnp.float32)
    inverse = jnp.exp(-(2.0 * half / width) * jnp.log(10000.0))
    angle = index[:, None] * inverse[None, :]
    return jnp.where((column % 2 == 0)[None, :], jnp.sin(angle), jnp.cos(angle))


def attend(queries, keys, values, grads):
    length = queries.shape[0]
    scale = HEAD_DIM ** (-0.5)
    block = 512 if length % 512 == 0 else length
    count = length // block

    def step(carry, index):
        key_acc, value_acc = carry
        start = index * block
        q_block = lax.dynamic_slice_in_dim(queries, start, block, 0)
        g_block = lax.dynamic_slice_in_dim(grads, start, block, 0)
        scores = (
            jnp.einsum("qhd,khd->hqk", q_block, keys, preferred_element_type=jnp.float32) * scale
        )
        top = jnp.max(scores, axis=-1, keepdims=True)
        expo = jnp.exp(scores - top)
        probs = expo / jnp.sum(expo, axis=-1, keepdims=True)
        weights = probs.astype(jnp.bfloat16)
        attended = jnp.einsum("hqk,khd->qhd", weights, values, preferred_element_type=jnp.float32)
        delta = jnp.sum(g_block.astype(jnp.float32) * attended, axis=-1)
        dprobs = jnp.einsum("qhd,khd->hqk", g_block, values, preferred_element_type=jnp.float32)
        dscores = (probs * (dprobs - jnp.transpose(delta)[:, :, None])).astype(jnp.bfloat16)
        grad_q = (
            jnp.einsum("hqk,khd->qhd", dscores, keys, preferred_element_type=jnp.float32) * scale
        ).astype(jnp.bfloat16)
        key_acc = key_acc + jnp.einsum(
            "hqk,qhd->khd", dscores, q_block, preferred_element_type=jnp.float32
        )
        value_acc = value_acc + jnp.einsum(
            "hqk,qhd->khd", weights, g_block, preferred_element_type=jnp.float32
        )
        return ((key_acc, value_acc), grad_q)

    zeros = jnp.zeros(keys.shape, jnp.float32)
    (key_acc, value_acc), grad_blocks = lax.scan(
        step, (zeros, zeros), jnp.arange(count, dtype=jnp.int32)
    )
    grad_q = grad_blocks.reshape(queries.shape)
    grad_k = (key_acc * scale).astype(jnp.bfloat16)
    grad_v = value_acc.astype(jnp.bfloat16)
    return (grad_q, grad_k, grad_v)


def weight_term(inputs, grad_qkv):
    return lax.dot_general(
        inputs, grad_qkv, (((0,), (0,)), ((), ())), preferred_element_type=jnp.float32
    )


def local(tokens, qkv_weight, grad_out, keep):
    local_tokens = tokens[0]
    local_grads = grad_out[0]
    rows = local_tokens.shape[0]
    width = local_tokens.shape[1]
    attw = qkv_weight.shape[1] // 3
    rowid = lax.axis_index("seq") * rows + jnp.arange(rows, dtype=jnp.int32)
    code = position_code(rowid, keep[0], width)
    inputs = (local_tokens.astype(jnp.float32) + code).astype(jnp.bfloat16)
    qkv = jnp.dot(inputs, qkv_weight, preferred_element_type=jnp.float32).astype(jnp.bfloat16)
    head_q, head_k, head_v, head_g = (
        lax.all_to_all(qkv[:, :attw], "seq", split_axis=1, concat_axis=0, tiled=True),
        lax.all_to_all(qkv[:, attw : 2 * attw], "seq", split_axis=1, concat_axis=0, tiled=True),
        lax.all_to_all(qkv[:, 2 * attw :], "seq", split_axis=1, concat_axis=0, tiled=True),
        lax.all_to_all(local_grads, "seq", split_axis=1, concat_axis=0, tiled=True),
    )
    length = head_q.shape[0]
    narrow = head_q.shape[1]
    shape = (length, narrow // HEAD_DIM, HEAD_DIM)
    grad_q, grad_k, grad_v = attend(
        head_q.reshape(shape), head_k.reshape(shape), head_v.reshape(shape), head_g.reshape(shape)
    )
    flat_q = grad_q.reshape(length, narrow)
    flat_k = grad_k.reshape(length, narrow)
    flat_v = grad_v.reshape(length, narrow)
    back_q, back_k, back_v = (
        lax.all_to_all(flat_q, "seq", split_axis=0, concat_axis=1, tiled=True),
        lax.all_to_all(flat_k, "seq", split_axis=0, concat_axis=1, tiled=True),
        lax.all_to_all(flat_v, "seq", split_axis=0, concat_axis=1, tiled=True),
    )
    grad_qkv = jnp.concatenate([back_q, back_k, back_v], axis=1)
    grad_tokens = jnp.dot(
        grad_qkv, jnp.transpose(qkv_weight), preferred_element_type=jnp.float32
    ).astype(jnp.bfloat16)
    partial_rows = lax.psum_scatter(
        weight_term(inputs, grad_qkv).astype(jnp.bfloat16), "seq", scatter_dimension=0, tiled=True
    )
    grad_weight = lax.psum_scatter(partial_rows, "dp", scatter_dimension=0, tiled=True).astype(
        jnp.float32
    )
    return (grad_tokens[None], grad_weight)


def solution(mesh):
    in_specs = (P("dp", "seq", None), P(), P("dp", "seq", None), P("dp", None))
    out_specs = (P("dp", "seq", None), P(("seq", "dp"), None))
    seq, dp = mesh.shape["seq"], mesh.shape["dp"]

    def device(tokens, qkv_weight, grad_out, keep):
        heads = qkv_weight.shape[1] // 3 // HEAD_DIM
        rows = tokens.shape[1]
        if seq == 4 and heads == 2 * seq and dp % 4 == 0 and rows % 64 == 0:
            return fused(dp // 2, tokens, qkv_weight, grad_out, keep)
        return local(tokens, qkv_weight, grad_out, keep)

    return jax.shard_map(device, mesh=mesh, in_specs=in_specs, out_specs=out_specs, check_vma=False)
```

```python
import functools

import numpy as np
import jax
import jax.numpy as jnp
from jax import lax
from jax.experimental import pallas as pl
from jax.experimental.pallas import tpu as pltpu
from jax.sharding import PartitionSpec as P

HEAD_DIM = 88
GRID = 1024
MESH = pl.DeviceIdType.MESH
LANES = 128
SINE = (
    6.283182793407034,
    -41.34141938561695,
    81.59613875537907,
    -76.57968785099001,
    41.203743633541215,
    -12.268859940824616,
)
NT = (((1,), (1,)), ((), ()))
NN = (((1,), (0,)), ((), ()))


def mm(a, b, dims=NN):
    return lax.dot_general(a, b, dims, preferred_element_type=jnp.float32)


def fused_kernel(
    nz, heads, tokens, weight, grads, keep, freq, phase, gt_out, last_in,
    x_all, g_send, g_all, w_own, w_all, qkv, x_t, dk_acc, dv_acc, d_own, d_back, d_cat,
    part, core_in, pair, z_in, run, total,
    w_sem, x_ss, x_rs, r_ss, r_rs, g_ss, g_rs, d_ss, d_rs, c_ss, c_rs, z_ss, z_rs, f_ss, f_rs,
):
    hd = HEAD_DIM
    pairw = 2 * hd
    rows, width = tokens.shape
    attw = weight.shape[0] // 3
    seq = heads // 2
    length = seq * rows
    own_rows = width // (seq * nz * 2)
    pad_rows = total.shape[1]
    cw = d_own.shape[1]
    visible = keep.shape[1]
    s = lax.axis_index("seq")
    d = lax.axis_index("dp")
    z = d // 2
    c = d % 2
    oc = 1 - c
    sib = z * 2 + oc
    peers = (s + 1 - 2 * (s % 2), (s + 2) % 4, 3 - s)
    zpeers = [(z + k) % nz for k in range(1, nz)]
    zsrcs = [(z + nz - k) % nz for k in range(1, nz)]

    def at_rows(who):
        return pl.ds(pl.multiple_of(who * rows, 64), rows)

    def send(src, dst, ss, rs, dev):
        copy = pltpu.make_async_remote_copy(
            src_ref=src, dst_ref=dst, send_sem=ss, recv_sem=rs,
            device_id=dev, device_id_type=MESH,
        )
        copy.start()
        return copy

    w_copies = [
        pltpu.make_async_copy(
            weight.at[pl.ds(pl.multiple_of(i * attw + s * pairw, 16), pairw)], w_own.at[i], w_sem.at[i]
        )
        for i in range(3)
    ]
    w_copies.append(pltpu.make_async_copy(weight, w_all, w_sem.at[3]))
    for copy in w_copies:
        copy.start()

    barrier = pltpu.get_barrier_semaphore()
    for p in peers:
        pl.semaphore_signal(barrier, inc=1, device_id=(p, d), device_id_type=MESH)
    pl.semaphore_signal(barrier, inc=1, device_id=(s, sib), device_id_type=MESH)
    for p in zpeers:
        pl.semaphore_signal(barrier, inc=1, device_id=(s, p * 2 + c), device_id_type=MESH)

    row = s * rows + lax.broadcasted_iota(jnp.int32, (rows, visible), 0)
    frame = row // visible
    slot = row - frame * visible
    lane = lax.broadcasted_iota(jnp.int32, (rows, visible), 1)
    spot = jnp.where(slot == lane, (frame * GRID + keep[...]).astype(jnp.float32), 0.0)
    index = jnp.sum(spot, axis=1, keepdims=True)
    mine = at_rows(s)
    half = rows // 2

    def half_of(who, i):
        return pl.ds(pl.multiple_of(who * rows + i * half, 32), half)

    for i in range(2):
        lo = i * half
        turns = index[lo : lo + half] * freq[...] + phase[...]
        r = turns - jnp.floor(turns + 0.5)
        r2 = r * r
        poly = jnp.full_like(r2, SINE[-1])
        for coef in SINE[-2::-1]:
            poly = poly * r2 + coef
        x = (tokens[lo : lo + half, :].astype(jnp.float32) + poly * r).astype(jnp.bfloat16)
        x_all[half_of(s, i), :] = x
    pl.semaphore_wait(barrier, 4 + nz - 1)
    x_copies = {}
    for k, i in ((0, 0), (1, 1), (0, 1), (1, 0)):
        where = x_all.at[half_of(s, i)]
        x_copies[k, i] = send(where, where, x_ss.at[k, i], x_rs.at[k, i], (peers[k], d))

    g_send[...] = jnp.zeros_like(g_send)
    for p in range(seq):
        for h in range(2):
            g_send[p, :, h * LANES : h * LANES + hd] = grads[:, p * pairw + h * hd : p * pairw + (h + 1) * hd]
    g_all[mine, :] = g_send[s]

    qkv[...] = jnp.zeros_like(qkv)
    for copy in w_copies[:3]:
        copy.wait()

    def project(who):
        x = x_all[at_rows(who), :]
        for i in range(3):
            out = mm(x, w_own[i], NT).astype(jnp.bfloat16)
            for h in range(2):
                to = (2 * i + h) * LANES
                qkv[at_rows(who), to : to + hd] = out[:, h * hd : (h + 1) * hd]

    def transpose(who):
        xt = x_all[at_rows(who), :].astype(jnp.float32).T
        for r in range(width // own_rows):
            t, zc = r // (2 * nz), r % (2 * nz)
            piece = xt[r * own_rows : (r + 1) * own_rows]
            piece = jnp.concatenate([piece, jnp.zeros((pad_rows - own_rows, rows), jnp.float32)], axis=0)
            to = (zc * seq + t) * pad_rows
            x_t[who, to : to + pad_rows, :] = piece.astype(jnp.bfloat16)

    project(s)
    relays = []
    for k in range(2):
        x_copies[k, k].wait_recv()
        where = x_all.at[half_of(peers[k], k)]
        relays.append(send(where, where, r_ss.at[k], r_rs.at[k], (peers[1 - k], d)))
    g_copies = [
        send(g_send.at[p], g_all.at[mine], g_ss.at[k], g_rs.at[k], (p, d)) for k, p in enumerate(peers)
    ]
    transpose(s)
    for k in range(2):
        x_copies[k, 1 - k].wait_recv()
        project(peers[k])
    for k in range(2):
        transpose(peers[k])
    for k in range(2):
        relays[k].wait_recv()
    project(peers[2])
    transpose(peers[2])
    for copy in g_copies:
        copy.wait_recv()

    block = 256 if length % 256 == 0 else rows
    scale = hd ** (-0.5)
    dk_acc[...] = jnp.zeros_like(dk_acc)
    dv_acc[...] = jnp.zeros_like(dv_acc)
    d_own[:, 512:] = jnp.zeros((length, cw - 512), jnp.bfloat16)

    def attention(b, carry):
        at = pl.ds(pl.multiple_of(b * block, block), block)
        for h in range(2):
            q = qkv[at, h * LANES : (h + 1) * LANES]
            g = g_all[at, h * LANES : (h + 1) * LANES]
            keys = qkv[:, (2 + h) * LANES : (3 + h) * LANES]
            values = qkv[:, (4 + h) * LANES : (5 + h) * LANES]
            st = mm(keys, q, NT)
            e = jnp.exp2((st - jnp.max(st, axis=0, keepdims=True)) * (scale * 1.4426950408889634))
            p = e * (1.0 / jnp.sum(e, axis=0, keepdims=True))
            w = p.astype(jnp.bfloat16)
            dp = mm(values, g, NT)
            delta = jnp.sum(w.astype(jnp.float32) * dp, axis=0, keepdims=True)
            ds = (p * (dp - delta)).astype(jnp.bfloat16)
            dv_acc[h] += mm(w, g)
            dk_acc[h] += mm(ds, q)
            dq = mm(keys.T, ds).T * scale
            d_own[at, h * hd : (h + 1) * hd] = dq[:, :hd].astype(jnp.bfloat16)
        return carry

    lax.fori_loop(0, length // block, attention, 0, unroll=True)
    for h in range(2):
        at = pairw + h * hd
        d_own[:, at : at + hd] = (dk_acc[h, :, :hd] * scale).astype(jnp.bfloat16)
        at = 2 * pairw + h * hd
        d_own[:, at : at + hd] = dv_acc[h, :, :hd].astype(jnp.bfloat16)

    d_copies = [
        send(d_own.at[at_rows(p)], d_back.at[s], d_ss.at[k], d_rs.at[k], (p, d)) for k, p in enumerate(peers)
    ]
    d_back[s] = d_own[mine, :]

    span = seq * pad_rows
    core_copies = []
    flip = z // (nz // 2)
    zm = z + flip * (nz - 1 - 2 * z)
    order = [p for k in range(nz // 2) for p in (nz - 1 - k, k)]

    def own_part(p):
        mine_part = part[p, pl.ds(pl.multiple_of(c * span, 64), span), :].astype(jnp.float32)
        return mine_part + core_in[p].astype(jnp.float32)

    def hop(p, way, to):
        return pltpu.make_async_remote_copy(
            src_ref=pair.at[p], dst_ref=z_in.at[way, p], send_sem=z_ss.at[p], recv_sem=z_rs.at[way, p],
            device_id=(s, to * 2 + c), device_id_type=MESH,
        )

    def pass_on(k):
        core_copies[k].wait_recv()
        p0 = order[k]
        p = p0 + flip * (nz - 1 - 2 * p0)

        @pl.when(p0 > zm)
        def _():
            onward = hop(p, flip, z + 1 - 2 * flip)
            run[...] = own_part(p)

            @pl.when(zm > 0)
            def _():
                onward.wait_recv()
                run[...] += z_in[flip, p].astype(jnp.float32)

            pair[p] = run[...].astype(jnp.bfloat16)
            onward.start()

        @pl.when(p0 < zm)
        def _():
            back = hop(p, 1 - flip, z - 1 + 2 * flip)
            back.wait_recv()
            pair[p] = (own_part(p) + z_in[1 - flip, p].astype(jnp.float32)).astype(jnp.bfloat16)
            back.start()

    for k, p0 in enumerate(order):
        p = p0 + flip * (nz - 1 - 2 * p0)
        chunk = pl.ds(pl.multiple_of(p * (2 * span), 128), 2 * span)
        acc = mm(x_t[0, chunk, :], d_own[0:rows, :])
        for q in range(1, seq):
            acc = acc + mm(x_t[q, chunk, :], d_own[q * rows : (q + 1) * rows, :])
        part[p] = acc.astype(jnp.bfloat16)
        other = part.at[p, pl.ds(pl.multiple_of(oc * span, 64), span)]
        core_copies.append(send(other, core_in.at[p], c_ss.at[k], c_rs.at[k], (s, sib)))
        if k > 0:
            pass_on(k - 1)
    pass_on(nz - 1)

    for copy in d_copies:
        copy.wait_recv()
    for p in range(seq):
        for i in range(3):
            at = i * attw + p * pairw
            d_cat[:, at : at + pairw] = d_back[p, :, i * pairw : (i + 1) * pairw]
    w_copies[3].wait()
    gt_out[...] = mm(d_cat[...], w_all[...]).astype(jnp.bfloat16)

    run[...] = own_part(z)

    @pl.when(z > 0)
    def _():
        hop(z, 0, (z + 1) % nz).wait_recv()
        run[...] += z_in[0, z].astype(jnp.float32)

    @pl.when(z < nz - 1)
    def _():
        hop(z, 1, (z + 1) % nz).wait_recv()
        run[...] += z_in[1, z].astype(jnp.float32)

    acc = run[...]
    acc = acc.astype(jnp.bfloat16)
    for t in range(seq):
        total[t] = acc[t * pad_rows : (t + 1) * pad_rows, :]
    f_copies = [send(total.at[p], last_in.at[s], f_ss.at[k], f_rs.at[k], (p, d)) for k, p in enumerate(peers)]
    last_in[s] = total[s]
    for copy in f_copies:
        copy.wait_recv()
    for copy in list(x_copies.values()) + relays + g_copies + d_copies + core_copies + f_copies:
        copy.wait_send()
    for p in zpeers:
        hop(p, 0, p).wait_send()


def finish_kernel(last_in, gt_in, gt_out, gw_out):
    gt_out[...] = gt_in[...]
    seq = last_in.shape[0]
    pairw = 2 * HEAD_DIM
    attw = gw_out.shape[1] // 3
    for p in range(seq):
        for i in range(3):
            at = i * attw + p * pairw
            piece = last_in[p, : gw_out.shape[0], i * pairw : (i + 1) * pairw]
            gw_out[:, at : at + pairw] = piece.astype(jnp.float32)


def fused(nz, tokens, qkv_weight, grad_out, keep):
    tokens, grad_out = tokens[0], grad_out[0]
    rows, width = tokens.shape
    cols = qkv_weight.shape[1]
    attw = cols // 3
    heads = attw // HEAD_DIM
    seq = heads // 2
    length = seq * rows
    own_rows = width // (seq * nz * 2)
    pad_rows = -(-own_rows // 16) * 16
    cw = -(-6 * HEAD_DIM // LANES) * LANES
    column = np.arange(width)
    freq = 10000.0 ** (-(2.0 * (column // 2)) / width) / (2.0 * np.pi)
    freq = jnp.asarray(freq[None, :].astype(np.float32))
    phase = jnp.asarray((0.25 * (column % 2))[None, :].astype(np.float32))
    bf16, f32 = jnp.bfloat16, jnp.float32
    vmem = pltpu.VMEM
    dma = pltpu.SemaphoreType.DMA
    scratch = [
        vmem((length, width), bf16),
        vmem((seq, rows, 2 * LANES), bf16),
        vmem((length, 2 * LANES), bf16),
        vmem((3, 2 * HEAD_DIM, width), bf16),
        vmem((cols, width), bf16),
        vmem((length, 6 * LANES), bf16),
        vmem((seq, 2 * nz * seq * pad_rows, rows), bf16),
        vmem((2, length, LANES), f32),
        vmem((2, length, LANES), f32),
        vmem((length, cw), bf16),
        vmem((seq, rows, cw), bf16),
        vmem((rows, cols), bf16),
        vmem((nz, 2 * seq * pad_rows, cw), bf16),
        vmem((nz, seq * pad_rows, cw), bf16),
        vmem((nz, seq * pad_rows, cw), bf16),
        vmem((2, nz, seq * pad_rows, cw), bf16),
        vmem((seq * pad_rows, cw), f32),
        vmem((seq, pad_rows, cw), bf16),
        dma((4,)), dma((2, 2)), dma((2, 2)), dma((2,)), dma((2,)),
        dma((3,)), dma((3,)), dma((3,)), dma((3,)), dma((nz,)), dma((nz,)),
        dma((nz,)), dma((2, nz)), dma((3,)), dma((3,)),
    ]
    whole = pl.BlockSpec(memory_space=pltpu.VMEM)
    gt, last = pl.pallas_call(
        functools.partial(fused_kernel, nz, heads),
        out_shape=[
            jax.ShapeDtypeStruct((rows, width), bf16),
            jax.ShapeDtypeStruct((seq, pad_rows, cw), bf16),
        ],
        in_specs=[whole, pl.BlockSpec(memory_space=pl.ANY)] + [whole] * 4,
        out_specs=[whole] * 2,
        scratch_shapes=scratch,
        compiler_params=pltpu.CompilerParams(
            collective_id=0, has_side_effects=True, vmem_limit_bytes=58 * 2**20
        ),
    )(tokens, qkv_weight.T, grad_out, keep, freq, phase)
    gt, gw = pl.pallas_call(
        finish_kernel,
        out_shape=[
            jax.ShapeDtypeStruct((rows, width), bf16),
            jax.ShapeDtypeStruct((own_rows, cols), f32),
        ],
        in_specs=[whole] * 2,
        out_specs=[whole] * 2,
    )(last, gt)
    return gt[None], gw


def position_code(rowid, keep_row, width):
    visible = keep_row.shape[0]
    frame = rowid // visible
    slot = rowid % visible
    onehot = slot[:, None] == jnp.arange(visible, dtype=jnp.int32)[None, :]
    spatial = jnp.sum(jnp.where(onehot, keep_row[None, :], 0), axis=1)
    index = (frame * GRID + spatial).astype(jnp.float32)
    column = jnp.arange(width, dtype=jnp.int32)
    half = (column // 2).astype(jnp.float32)
    inverse = jnp.exp(-(2.0 * half / width) * jnp.log(10000.0))
    angle = index[:, None] * inverse[None, :]
    return jnp.where((column % 2 == 0)[None, :], jnp.sin(angle), jnp.cos(angle))


def attend(queries, keys, values, grads):
    length = queries.shape[0]
    scale = HEAD_DIM ** (-0.5)
    block = 512 if length % 512 == 0 else length
    count = length // block

    def step(carry, index):
        key_acc, value_acc = carry
        start = index * block
        q_block = lax.dynamic_slice_in_dim(queries, start, block, 0)
        g_block = lax.dynamic_slice_in_dim(grads, start, block, 0)
        scores = (
            jnp.einsum("qhd,khd->hqk", q_block, keys, preferred_element_type=jnp.float32) * scale
        )
        top = jnp.max(scores, axis=-1, keepdims=True)
        expo = jnp.exp(scores - top)
        probs = expo / jnp.sum(expo, axis=-1, keepdims=True)
        weights = probs.astype(jnp.bfloat16)
        attended = jnp.einsum("hqk,khd->qhd", weights, values, preferred_element_type=jnp.float32)
        delta = jnp.sum(g_block.astype(jnp.float32) * attended, axis=-1)
        dprobs = jnp.einsum("qhd,khd->hqk", g_block, values, preferred_element_type=jnp.float32)
        dscores = (probs * (dprobs - jnp.transpose(delta)[:, :, None])).astype(jnp.bfloat16)
        grad_q = (
            jnp.einsum("hqk,khd->qhd", dscores, keys, preferred_element_type=jnp.float32) * scale
        ).astype(jnp.bfloat16)
        key_acc = key_acc + jnp.einsum(
            "hqk,qhd->khd", dscores, q_block, preferred_element_type=jnp.float32
        )
        value_acc = value_acc + jnp.einsum(
            "hqk,qhd->khd", weights, g_block, preferred_element_type=jnp.float32
        )
        return ((key_acc, value_acc), grad_q)

    zeros = jnp.zeros(keys.shape, jnp.float32)
    (key_acc, value_acc), grad_blocks = lax.scan(
        step, (zeros, zeros), jnp.arange(count, dtype=jnp.int32)
    )
    grad_q = grad_blocks.reshape(queries.shape)
    grad_k = (key_acc * scale).astype(jnp.bfloat16)
    grad_v = value_acc.astype(jnp.bfloat16)
    return (grad_q, grad_k, grad_v)


def weight_term(inputs, grad_qkv):
    return lax.dot_general(
        inputs, grad_qkv, (((0,), (0,)), ((), ())), preferred_element_type=jnp.float32
    )


def local(tokens, qkv_weight, grad_out, keep):
    local_tokens = tokens[0]
    local_grads = grad_out[0]
    rows = local_tokens.shape[0]
    width = local_tokens.shape[1]
    attw = qkv_weight.shape[1] // 3
    rowid = lax.axis_index("seq") * rows + jnp.arange(rows, dtype=jnp.int32)
    code = position_code(rowid, keep[0], width)
    inputs = (local_tokens.astype(jnp.float32) + code).astype(jnp.bfloat16)
    qkv = jnp.dot(inputs, qkv_weight, preferred_element_type=jnp.float32).astype(jnp.bfloat16)
    head_q, head_k, head_v, head_g = (
        lax.all_to_all(qkv[:, :attw], "seq", split_axis=1, concat_axis=0, tiled=True),
        lax.all_to_all(qkv[:, attw : 2 * attw], "seq", split_axis=1, concat_axis=0, tiled=True),
        lax.all_to_all(qkv[:, 2 * attw :], "seq", split_axis=1, concat_axis=0, tiled=True),
        lax.all_to_all(local_grads, "seq", split_axis=1, concat_axis=0, tiled=True),
    )
    length = head_q.shape[0]
    narrow = head_q.shape[1]
    shape = (length, narrow // HEAD_DIM, HEAD_DIM)
    grad_q, grad_k, grad_v = attend(
        head_q.reshape(shape), head_k.reshape(shape), head_v.reshape(shape), head_g.reshape(shape)
    )
    flat_q = grad_q.reshape(length, narrow)
    flat_k = grad_k.reshape(length, narrow)
    flat_v = grad_v.reshape(length, narrow)
    back_q, back_k, back_v = (
        lax.all_to_all(flat_q, "seq", split_axis=0, concat_axis=1, tiled=True),
        lax.all_to_all(flat_k, "seq", split_axis=0, concat_axis=1, tiled=True),
        lax.all_to_all(flat_v, "seq", split_axis=0, concat_axis=1, tiled=True),
    )
    grad_qkv = jnp.concatenate([back_q, back_k, back_v], axis=1)
    grad_tokens = jnp.dot(
        grad_qkv, jnp.transpose(qkv_weight), preferred_element_type=jnp.float32
    ).astype(jnp.bfloat16)
    partial_rows = lax.psum_scatter(
        weight_term(inputs, grad_qkv).astype(jnp.bfloat16), "seq", scatter_dimension=0, tiled=True
    )
    grad_weight = lax.psum_scatter(partial_rows, "dp", scatter_dimension=0, tiled=True).astype(
        jnp.float32
    )
    return (grad_tokens[None], grad_weight)


def solution(mesh):
    in_specs = (P("dp", "seq", None), P(), P("dp", "seq", None), P("dp", None))
    out_specs = (P("dp", "seq", None), P(("seq", "dp"), None))
    seq, dp = mesh.shape["seq"], mesh.shape["dp"]

    def device(tokens, qkv_weight, grad_out, keep):
        heads = qkv_weight.shape[1] // 3 // HEAD_DIM
        rows = tokens.shape[1]
        if seq == 4 and heads == 2 * seq and dp % 4 == 0 and rows % 64 == 0:
            return fused(dp // 2, tokens, qkv_weight, grad_out, keep)
        return local(tokens, qkv_weight, grad_out, keep)

    return jax.shard_map(device, mesh=mesh, in_specs=in_specs, out_specs=out_specs, check_vma=False)
```

```python
import functools

import numpy as np
import jax
import jax.numpy as jnp
from jax import lax
from jax.experimental import pallas as pl
from jax.experimental.pallas import tpu as pltpu
from jax.sharding import PartitionSpec as P

HEAD_DIM = 88
GRID = 1024
MESH = pl.DeviceIdType.MESH
LANES = 128
SINE = (
    6.283182793407034,
    -41.34141938561695,
    81.59613875537907,
    -76.57968785099001,
    41.203743633541215,
    -12.268859940824616,
)
NT = (((1,), (1,)), ((), ()))
NN = (((1,), (0,)), ((), ()))


def mm(a, b, dims=NN):
    return lax.dot_general(a, b, dims, preferred_element_type=jnp.float32)


def fused_kernel(
    nz, heads, tokens, weight, grads, keep, freq, phase, gt_out, last_in,
    x_all, g_send, g_all, w_own, w_all, qkv, x_t, dk_acc, dv_acc, d_own, d_back, d_cat,
    part, core_in, pair, z_in, run, total,
    w_sem, x_ss, x_rs, r_ss, r_rs, g_ss, g_rs, d_ss, d_rs, c_ss, c_rs, z_ss, z_rs, f_ss, f_rs,
):
    hd = HEAD_DIM
    pairw = 2 * hd
    rows, width = tokens.shape
    attw = weight.shape[0] // 3
    seq = heads // 2
    length = seq * rows
    own_rows = width // (seq * nz * 2)
    pad_rows = total.shape[1]
    cw = d_own.shape[1]
    visible = keep.shape[1]
    s = lax.axis_index("seq")
    d = lax.axis_index("dp")
    z = d // 2
    c = d % 2
    oc = 1 - c
    sib = z * 2 + oc
    peers = (s + 1 - 2 * (s % 2), (s + 2) % 4, 3 - s)
    zpeers = [(z + k) % nz for k in range(1, nz)]
    zsrcs = [(z + nz - k) % nz for k in range(1, nz)]

    def at_rows(who):
        return pl.ds(pl.multiple_of(who * rows, 64), rows)

    def send(src, dst, ss, rs, dev):
        copy = pltpu.make_async_remote_copy(
            src_ref=src, dst_ref=dst, send_sem=ss, recv_sem=rs,
            device_id=dev, device_id_type=MESH,
        )
        copy.start()
        return copy

    w_copies = [
        pltpu.make_async_copy(
            weight.at[pl.ds(pl.multiple_of(i * attw + s * pairw, 16), pairw)], w_own.at[i], w_sem.at[i]
        )
        for i in range(3)
    ]
    w_copies.append(pltpu.make_async_copy(weight, w_all, w_sem.at[3]))
    for copy in w_copies:
        copy.start()

    barrier = pltpu.get_barrier_semaphore()
    for p in peers:
        pl.semaphore_signal(barrier, inc=1, device_id=(p, d), device_id_type=MESH)
    pl.semaphore_signal(barrier, inc=1, device_id=(s, sib), device_id_type=MESH)
    for p in zpeers:
        pl.semaphore_signal(barrier, inc=1, device_id=(s, p * 2 + c), device_id_type=MESH)

    row = s * rows + lax.broadcasted_iota(jnp.int32, (rows, visible), 0)
    frame = row // visible
    slot = row - frame * visible
    lane = lax.broadcasted_iota(jnp.int32, (rows, visible), 1)
    spot = jnp.where(slot == lane, (frame * GRID + keep[...]).astype(jnp.float32), 0.0)
    index = jnp.sum(spot, axis=1, keepdims=True)
    mine = at_rows(s)
    half = rows // 2

    def half_of(who, i):
        return pl.ds(pl.multiple_of(who * rows + i * half, 32), half)

    for i in range(2):
        lo = i * half
        turns = index[lo : lo + half] * freq[...] + phase[...]
        r = turns - jnp.floor(turns + 0.5)
        r2 = r * r
        poly = jnp.full_like(r2, SINE[-1])
        for coef in SINE[-2::-1]:
            poly = poly * r2 + coef
        x = (tokens[lo : lo + half, :].astype(jnp.float32) + poly * r).astype(jnp.bfloat16)
        x_all[half_of(s, i), :] = x
    pl.semaphore_wait(barrier, 4 + nz - 1)
    x_copies = {}
    for k, i in ((0, 0), (1, 1), (0, 1), (1, 0)):
        where = x_all.at[half_of(s, i)]
        x_copies[k, i] = send(where, where, x_ss.at[k, i], x_rs.at[k, i], (peers[k], d))

    g_send[...] = jnp.zeros_like(g_send)
    for p in range(seq):
        for h in range(2):
            g_send[p, :, h * LANES : h * LANES + hd] = grads[:, p * pairw + h * hd : p * pairw + (h + 1) * hd]
    g_all[mine, :] = g_send[s]

    qkv[...] = jnp.zeros_like(qkv)
    for copy in w_copies[:3]:
        copy.wait()

    def project(who):
        x = x_all[at_rows(who), :]
        for i in range(3):
            out = mm(x, w_own[i], NT).astype(jnp.bfloat16)
            for h in range(2):
                to = (2 * i + h) * LANES
                qkv[at_rows(who), to : to + hd] = out[:, h * hd : (h + 1) * hd]

    def transpose(who):
        xt = x_all[at_rows(who), :].T.astype(jnp.float32)
        for r in range(width // own_rows):
            t, zc = r // (2 * nz), r % (2 * nz)
            piece = xt[r * own_rows : (r + 1) * own_rows]
            piece = jnp.concatenate([piece, jnp.zeros((pad_rows - own_rows, rows), jnp.float32)], axis=0)
            to = (zc * seq + t) * pad_rows
            x_t[who, to : to + pad_rows, :] = piece.astype(jnp.bfloat16)

    project(s)
    relays = []
    for k in range(2):
        x_copies[k, k].wait_recv()
        where = x_all.at[half_of(peers[k], k)]
        relays.append(send(where, where, r_ss.at[k], r_rs.at[k], (peers[1 - k], d)))
    g_copies = [
        send(g_send.at[p], g_all.at[mine], g_ss.at[k], g_rs.at[k], (p, d)) for k, p in enumerate(peers)
    ]
    transpose(s)
    for k in range(2):
        x_copies[k, 1 - k].wait_recv()
        project(peers[k])
    for k in range(2):
        transpose(peers[k])
    for k in range(2):
        relays[k].wait_recv()
    project(peers[2])
    transpose(peers[2])
    for copy in g_copies:
        copy.wait_recv()

    block = 256 if length % 256 == 0 else rows
    scale = hd ** (-0.5)
    dk_acc[...] = jnp.zeros_like(dk_acc)
    dv_acc[...] = jnp.zeros_like(dv_acc)
    d_own[:, 512:] = jnp.zeros((length, cw - 512), jnp.bfloat16)

    def attention(b, carry):
        at = pl.ds(pl.multiple_of(b * block, block), block)
        for h in range(2):
            q = qkv[at, h * LANES : (h + 1) * LANES]
            g = g_all[at, h * LANES : (h + 1) * LANES]
            keys = qkv[:, (2 + h) * LANES : (3 + h) * LANES]
            values = qkv[:, (4 + h) * LANES : (5 + h) * LANES]
            st = mm(keys, q, NT)
            e = jnp.exp2((st - jnp.max(st, axis=0, keepdims=True)) * (scale * 1.4426950408889634))
            p = e * (1.0 / jnp.sum(e, axis=0, keepdims=True))
            w = p.astype(jnp.bfloat16)
            dp = mm(values, g, NT)
            delta = jnp.sum(w.astype(jnp.float32) * dp, axis=0, keepdims=True)
            ds = (p * (dp - delta)).astype(jnp.bfloat16)
            dv_acc[h] += mm(w, g)
            dk_acc[h] += mm(ds, q)
            dq = mm(keys.T, ds).T * scale
            d_own[at, h * hd : (h + 1) * hd] = dq[:, :hd].astype(jnp.bfloat16)
        return carry

    lax.fori_loop(0, length // block, attention, 0, unroll=True)
    for h in range(2):
        at = pairw + h * hd
        d_own[:, at : at + hd] = (dk_acc[h, :, :hd] * scale).astype(jnp.bfloat16)
        at = 2 * pairw + h * hd
        d_own[:, at : at + hd] = dv_acc[h, :, :hd].astype(jnp.bfloat16)

    d_copies = [
        send(d_own.at[at_rows(p)], d_back.at[s], d_ss.at[k], d_rs.at[k], (p, d)) for k, p in enumerate(peers)
    ]
    d_back[s] = d_own[mine, :]

    span = seq * pad_rows
    core_copies = []
    flip = z // (nz // 2)
    zm = z + flip * (nz - 1 - 2 * z)
    order = [p for k in range(nz // 2) for p in (nz - 1 - k, k)]

    def own_part(p):
        mine_part = part[p, pl.ds(pl.multiple_of(c * span, 64), span), :].astype(jnp.float32)
        return mine_part + core_in[p].astype(jnp.float32)

    def hop(p, way, to):
        return pltpu.make_async_remote_copy(
            src_ref=pair.at[p], dst_ref=z_in.at[way, p], send_sem=z_ss.at[p], recv_sem=z_rs.at[way, p],
            device_id=(s, to * 2 + c), device_id_type=MESH,
        )

    def pass_on(k):
        core_copies[k].wait_recv()
        p0 = order[k]
        p = p0 + flip * (nz - 1 - 2 * p0)

        @pl.when(p0 > zm)
        def _():
            onward = hop(p, flip, z + 1 - 2 * flip)
            run[...] = own_part(p)

            @pl.when(zm > 0)
            def _():
                onward.wait_recv()
                run[...] += z_in[flip, p].astype(jnp.float32)

            pair[p] = run[...].astype(jnp.bfloat16)
            onward.start()

        @pl.when(p0 < zm)
        def _():
            back = hop(p, 1 - flip, z - 1 + 2 * flip)
            back.wait_recv()
            pair[p] = (own_part(p) + z_in[1 - flip, p].astype(jnp.float32)).astype(jnp.bfloat16)
            back.start()

    for k, p0 in enumerate(order):
        p = p0 + flip * (nz - 1 - 2 * p0)
        chunk = pl.ds(pl.multiple_of(p * (2 * span), 128), 2 * span)
        acc = mm(x_t[0, chunk, :], d_own[0:rows, :])
        for q in range(1, seq):
            acc = acc + mm(x_t[q, chunk, :], d_own[q * rows : (q + 1) * rows, :])
        part[p] = acc.astype(jnp.bfloat16)
        other = part.at[p, pl.ds(pl.multiple_of(oc * span, 64), span)]
        core_copies.append(send(other, core_in.at[p], c_ss.at[k], c_rs.at[k], (s, sib)))
        if k > 0:
            pass_on(k - 1)
    pass_on(nz - 1)

    for copy in d_copies:
        copy.wait_recv()
    for p in range(seq):
        for i in range(3):
            at = i * attw + p * pairw
            d_cat[:, at : at + pairw] = d_back[p, :, i * pairw : (i + 1) * pairw]
    w_copies[3].wait()
    gt_out[...] = mm(d_cat[...], w_all[...]).astype(jnp.bfloat16)

    run[...] = own_part(z)

    @pl.when(z > 0)
    def _():
        hop(z, 0, (z + 1) % nz).wait_recv()
        run[...] += z_in[0, z].astype(jnp.float32)

    @pl.when(z < nz - 1)
    def _():
        hop(z, 1, (z + 1) % nz).wait_recv()
        run[...] += z_in[1, z].astype(jnp.float32)

    acc = run[...]
    acc = acc.astype(jnp.bfloat16)
    for t in range(seq):
        total[t] = acc[t * pad_rows : (t + 1) * pad_rows, :]
    f_copies = [send(total.at[p], last_in.at[s], f_ss.at[k], f_rs.at[k], (p, d)) for k, p in enumerate(peers)]
    last_in[s] = total[s]
    for copy in f_copies:
        copy.wait_recv()
    for copy in list(x_copies.values()) + relays + g_copies + d_copies + core_copies + f_copies:
        copy.wait_send()
    for p in zpeers:
        hop(p, 0, p).wait_send()


def finish_kernel(last_in, gt_in, gt_out, gw_out):
    gt_out[...] = gt_in[...]
    seq = last_in.shape[0]
    pairw = 2 * HEAD_DIM
    attw = gw_out.shape[1] // 3
    for p in range(seq):
        for i in range(3):
            at = i * attw + p * pairw
            piece = last_in[p, : gw_out.shape[0], i * pairw : (i + 1) * pairw]
            gw_out[:, at : at + pairw] = piece.astype(jnp.float32)


def fused(nz, tokens, qkv_weight, grad_out, keep):
    tokens, grad_out = tokens[0], grad_out[0]
    rows, width = tokens.shape
    cols = qkv_weight.shape[1]
    attw = cols // 3
    heads = attw // HEAD_DIM
    seq = heads // 2
    length = seq * rows
    own_rows = width // (seq * nz * 2)
    pad_rows = -(-own_rows // 16) * 16
    cw = -(-6 * HEAD_DIM // LANES) * LANES
    column = np.arange(width)
    freq = 10000.0 ** (-(2.0 * (column // 2)) / width) / (2.0 * np.pi)
    freq = jnp.asarray(freq[None, :].astype(np.float32))
    phase = jnp.asarray((0.25 * (column % 2))[None, :].astype(np.float32))
    bf16, f32 = jnp.bfloat16, jnp.float32
    vmem = pltpu.VMEM
    dma = pltpu.SemaphoreType.DMA
    scratch = [
        vmem((length, width), bf16),
        vmem((seq, rows, 2 * LANES), bf16),
        vmem((length, 2 * LANES), bf16),
        vmem((3, 2 * HEAD_DIM, width), bf16),
        vmem((cols, width), bf16),
        vmem((length, 6 * LANES), bf16),
        vmem((seq, 2 * nz * seq * pad_rows, rows), bf16),
        vmem((2, length, LANES), f32),
        vmem((2, length, LANES), f32),
        vmem((length, cw), bf16),
        vmem((seq, rows, cw), bf16),
        vmem((rows, cols), bf16),
        vmem((nz, 2 * seq * pad_rows, cw), bf16),
        vmem((nz, seq * pad_rows, cw), bf16),
        vmem((nz, seq * pad_rows, cw), bf16),
        vmem((2, nz, seq * pad_rows, cw), bf16),
        vmem((seq * pad_rows, cw), f32),
        vmem((seq, pad_rows, cw), bf16),
        dma((4,)), dma((2, 2)), dma((2, 2)), dma((2,)), dma((2,)),
        dma((3,)), dma((3,)), dma((3,)), dma((3,)), dma((nz,)), dma((nz,)),
        dma((nz,)), dma((2, nz)), dma((3,)), dma((3,)),
    ]
    whole = pl.BlockSpec(memory_space=pltpu.VMEM)
    gt, last = pl.pallas_call(
        functools.partial(fused_kernel, nz, heads),
        out_shape=[
            jax.ShapeDtypeStruct((rows, width), bf16),
            jax.ShapeDtypeStruct((seq, pad_rows, cw), bf16),
        ],
        in_specs=[whole, pl.BlockSpec(memory_space=pl.ANY)] + [whole] * 4,
        out_specs=[whole] * 2,
        scratch_shapes=scratch,
        compiler_params=pltpu.CompilerParams(
            collective_id=0, has_side_effects=True, vmem_limit_bytes=58 * 2**20
        ),
    )(tokens, qkv_weight.T, grad_out, keep, freq, phase)
    gt, gw = pl.pallas_call(
        finish_kernel,
        out_shape=[
            jax.ShapeDtypeStruct((rows, width), bf16),
            jax.ShapeDtypeStruct((own_rows, cols), f32),
        ],
        in_specs=[whole] * 2,
        out_specs=[whole] * 2,
    )(last, gt)
    return gt[None], gw


def position_code(rowid, keep_row, width):
    visible = keep_row.shape[0]
    frame = rowid // visible
    slot = rowid % visible
    onehot = slot[:, None] == jnp.arange(visible, dtype=jnp.int32)[None, :]
    spatial = jnp.sum(jnp.where(onehot, keep_row[None, :], 0), axis=1)
    index = (frame * GRID + spatial).astype(jnp.float32)
    column = jnp.arange(width, dtype=jnp.int32)
    half = (column // 2).astype(jnp.float32)
    inverse = jnp.exp(-(2.0 * half / width) * jnp.log(10000.0))
    angle = index[:, None] * inverse[None, :]
    return jnp.where((column % 2 == 0)[None, :], jnp.sin(angle), jnp.cos(angle))


def attend(queries, keys, values, grads):
    length = queries.shape[0]
    scale = HEAD_DIM ** (-0.5)
    block = 512 if length % 512 == 0 else length
    count = length // block

    def step(carry, index):
        key_acc, value_acc = carry
        start = index * block
        q_block = lax.dynamic_slice_in_dim(queries, start, block, 0)
        g_block = lax.dynamic_slice_in_dim(grads, start, block, 0)
        scores = (
            jnp.einsum("qhd,khd->hqk", q_block, keys, preferred_element_type=jnp.float32) * scale
        )
        top = jnp.max(scores, axis=-1, keepdims=True)
        expo = jnp.exp(scores - top)
        probs = expo / jnp.sum(expo, axis=-1, keepdims=True)
        weights = probs.astype(jnp.bfloat16)
        attended = jnp.einsum("hqk,khd->qhd", weights, values, preferred_element_type=jnp.float32)
        delta = jnp.sum(g_block.astype(jnp.float32) * attended, axis=-1)
        dprobs = jnp.einsum("qhd,khd->hqk", g_block, values, preferred_element_type=jnp.float32)
        dscores = (probs * (dprobs - jnp.transpose(delta)[:, :, None])).astype(jnp.bfloat16)
        grad_q = (
            jnp.einsum("hqk,khd->qhd", dscores, keys, preferred_element_type=jnp.float32) * scale
        ).astype(jnp.bfloat16)
        key_acc = key_acc + jnp.einsum(
            "hqk,qhd->khd", dscores, q_block, preferred_element_type=jnp.float32
        )
        value_acc = value_acc + jnp.einsum(
            "hqk,qhd->khd", weights, g_block, preferred_element_type=jnp.float32
        )
        return ((key_acc, value_acc), grad_q)

    zeros = jnp.zeros(keys.shape, jnp.float32)
    (key_acc, value_acc), grad_blocks = lax.scan(
        step, (zeros, zeros), jnp.arange(count, dtype=jnp.int32)
    )
    grad_q = grad_blocks.reshape(queries.shape)
    grad_k = (key_acc * scale).astype(jnp.bfloat16)
    grad_v = value_acc.astype(jnp.bfloat16)
    return (grad_q, grad_k, grad_v)


def weight_term(inputs, grad_qkv):
    return lax.dot_general(
        inputs, grad_qkv, (((0,), (0,)), ((), ())), preferred_element_type=jnp.float32
    )


def local(tokens, qkv_weight, grad_out, keep):
    local_tokens = tokens[0]
    local_grads = grad_out[0]
    rows = local_tokens.shape[0]
    width = local_tokens.shape[1]
    attw = qkv_weight.shape[1] // 3
    rowid = lax.axis_index("seq") * rows + jnp.arange(rows, dtype=jnp.int32)
    code = position_code(rowid, keep[0], width)
    inputs = (local_tokens.astype(jnp.float32) + code).astype(jnp.bfloat16)
    qkv = jnp.dot(inputs, qkv_weight, preferred_element_type=jnp.float32).astype(jnp.bfloat16)
    head_q, head_k, head_v, head_g = (
        lax.all_to_all(qkv[:, :attw], "seq", split_axis=1, concat_axis=0, tiled=True),
        lax.all_to_all(qkv[:, attw : 2 * attw], "seq", split_axis=1, concat_axis=0, tiled=True),
        lax.all_to_all(qkv[:, 2 * attw :], "seq", split_axis=1, concat_axis=0, tiled=True),
        lax.all_to_all(local_grads, "seq", split_axis=1, concat_axis=0, tiled=True),
    )
    length = head_q.shape[0]
    narrow = head_q.shape[1]
    shape = (length, narrow // HEAD_DIM, HEAD_DIM)
    grad_q, grad_k, grad_v = attend(
        head_q.reshape(shape), head_k.reshape(shape), head_v.reshape(shape), head_g.reshape(shape)
    )
    flat_q = grad_q.reshape(length, narrow)
    flat_k = grad_k.reshape(length, narrow)
    flat_v = grad_v.reshape(length, narrow)
    back_q, back_k, back_v = (
        lax.all_to_all(flat_q, "seq", split_axis=0, concat_axis=1, tiled=True),
        lax.all_to_all(flat_k, "seq", split_axis=0, concat_axis=1, tiled=True),
        lax.all_to_all(flat_v, "seq", split_axis=0, concat_axis=1, tiled=True),
    )
    grad_qkv = jnp.concatenate([back_q, back_k, back_v], axis=1)
    grad_tokens = jnp.dot(
        grad_qkv, jnp.transpose(qkv_weight), preferred_element_type=jnp.float32
    ).astype(jnp.bfloat16)
    partial_rows = lax.psum_scatter(
        weight_term(inputs, grad_qkv).astype(jnp.bfloat16), "seq", scatter_dimension=0, tiled=True
    )
    grad_weight = lax.psum_scatter(partial_rows, "dp", scatter_dimension=0, tiled=True).astype(
        jnp.float32
    )
    return (grad_tokens[None], grad_weight)


def solution(mesh):
    in_specs = (P("dp", "seq", None), P(), P("dp", "seq", None), P("dp", None))
    out_specs = (P("dp", "seq", None), P(("seq", "dp"), None))
    seq, dp = mesh.shape["seq"], mesh.shape["dp"]

    def device(tokens, qkv_weight, grad_out, keep):
        heads = qkv_weight.shape[1] // 3 // HEAD_DIM
        rows = tokens.shape[1]
        if seq == 4 and heads == 2 * seq and dp % 4 == 0 and rows % 64 == 0:
            return fused(dp // 2, tokens, qkv_weight, grad_out, keep)
        return local(tokens, qkv_weight, grad_out, keep)

    return jax.shard_map(device, mesh=mesh, in_specs=in_specs, out_specs=out_specs, check_vma=False)
```
